128 devices in a mesh: days: 2 (over x_lo), chan: 64 (over z, y, x_hi, core).
Axes of the slice: x: 4 (x_hi: 2, x_lo: 2; x = x_hi * 2 + x_lo), y: 4, z: 4, core: 2. Of those that a mesh axis runs over, the one named last changes fastest.
Arguments:
- spectra: bfloat16 [8, 512, 8192], P('days', None, 'chan'), may hold values from -6 to 6
- sources: int32 [2], replicated, may hold values from 0 to 8191
- offsets: int32 [8192], P('chan'), may hold values from 0 to 4095
Outputs:
- slant: float32 [128, 2, 2, 256], P('chan')
The draws below stay inside these ranges and needn't reach their ends.
All inputs are finite; a program needn't handle non-finite values.
Results may differ from the reference program's by a relative error of at most 0.0055.
Values may be sent and summed in bfloat16 or wider, within the bound.
No kernel may reach another device: no remote copies, remote signals or barrier semaphores. Data moves between devices by JAX's collectives and lax.ppermute only.
A program may use at most 64 MiB of HBM per device.

```python
import math
import jax
import jax.numpy as jnp
from jax import lax

BINS = 256
LAGS = 512
NSLOW = 128
NSRC = 2
CHANNELS = 8192
WINDOWS = 8


def touch_ends(array, key, low, top_value):
    shape = array.shape
    place = [jax.random.randint(jax.random.fold_in(key, axis), (), 0, shape[axis]) for axis in range(len(shape))]
    array = array.at[tuple(place)].set(low)
    longest = shape.index(max(shape))
    place[longest] = (place[longest] + 1) % shape[longest]
    return array.at[tuple(place)].set(top_value)


def block_levels(own_key, dims, shards, smallest, largest):
    level, own = 1.0, jax.random.fold_in(own_key, 6)
    for position, shards_of in shards:
        steps = jnp.exp(jax.random.uniform(jax.random.fold_in(own, position), (shards_of,), jnp.float32, smallest / len(shards), largest / len(shards)))
        level = level * jnp.repeat(steps, dims[position] // shards_of).reshape([-1 if axis == position else 1 for axis in range(len(dims))])
    return level


def noise(own_key, shape, spread, reach, cuts=(), kind=jnp.bfloat16):
    loudness = block_levels(own_key, shape, cuts, -0.22, 0.18) if cuts else 1.0
    result = jax.random.normal(own_key, shape, jnp.float32) * spread * loudness
    return jnp.minimum(jnp.maximum(result, -reach), reach).astype(kind)


def setup_inputs(seed: int = 0) -> dict:
    key_of = jax.random.split(jax.random.key(seed), 4)
    spectra = noise(key_of[0], (WINDOWS, 2 * BINS, CHANNELS), 1.0, 6.0, ((0, 2), (2, 64)))
    sources = jax.random.randint(key_of[1], (NSRC,), 0, CHANNELS).astype(jnp.int32)
    offsets = touch_ends(jax.random.randint(key_of[2], (CHANNELS,), 0, 4096), jax.random.fold_in(key_of[2], 1), 0, 4095).astype(jnp.int32)
    return {"spectra": spectra, "sources": sources, "offsets": offsets}


def angles(left_index, right_index, period):
    return (left_index * right_index % period).astype(jnp.float32) * (2.0 * math.pi / period)

def inverse_table(bins):
    lag_total = 2 * bins
    theta = angles(jnp.arange(lag_total, dtype=jnp.int32)[:, None], jnp.arange(bins, dtype=jnp.int32)[None, :], lag_total)
    cosine = jnp.cos(theta)
    sine = jnp.sin(theta)
    upper = jnp.concatenate([cosine, -sine], 1)
    lower = jnp.concatenate([sine, cosine], 1)
    return (jnp.concatenate([upper, lower], 0) / math.sqrt(bins)).astype(jnp.bfloat16)

def forward_table(bins, lag_first, lag_count):
    lag_total = 2 * bins
    theta = angles(jnp.arange(bins, dtype=jnp.int32)[:, None], lag_first + jnp.arange(lag_count, dtype=jnp.int32)[None, :], lag_total)
    return jnp.concatenate([jnp.cos(theta), -jnp.sin(theta)], 0) / math.sqrt(lag_total)

def slant_block(spec_re, spec_im, slowness, offsets, bins):
    freq = jnp.arange(bins, dtype=jnp.int32)
    phase = freq[None, :, None] * slowness[:, None, None] % 4096 * offsets[None, None, :] % 4096
    theta = phase.astype(jnp.float32) * (2.0 * math.pi / 4096)
    cosine = jnp.cos(theta)
    sine = jnp.sin(theta)
    highest = lax.Precision.HIGHEST
    real_part = jnp.einsum('sfc,kfc->ksf', spec_re, cosine, precision=highest) - jnp.einsum('sfc,kfc->ksf', spec_im, sine, precision=highest)
    imag_part = jnp.einsum('sfc,kfc->ksf', spec_re, sine, precision=highest) + jnp.einsum('sfc,kfc->ksf', spec_im, cosine, precision=highest)
    return jnp.stack([real_part, imag_part], 2)

def reference(spectra, sources, offsets):
    inverse = inverse_table(BINS).astype(jnp.float32)
    highest = lax.Precision.HIGHEST

    def one_window(totals, window):
        source_part = window[:, sources].T.astype(jnp.float32)
        channel_part = window.astype(jnp.float32)
        real_s = source_part[:, :BINS, None]
        imag_s = source_part[:, BINS:, None]
        real_x = channel_part[None, :BINS]
        imag_x = channel_part[None, BINS:]
        product = jnp.concatenate([real_s * real_x + imag_s * imag_x, real_s * imag_x - imag_s * real_x], 1)
        rounded = lax.optimization_barrier(product.astype(jnp.bfloat16)).astype(jnp.float32)
        analytic = jnp.einsum('lk,skc->slc', inverse, rounded, precision=highest)
        correlation = analytic[:, :LAGS]
        hilbert = analytic[:, LAGS:]
        magnitude = jnp.maximum(jnp.sqrt(correlation * correlation + hilbert * hilbert), 0.5)
        return ((totals[0] + correlation, totals[1] + correlation / magnitude, totals[2] + hilbert / magnitude), None)
    empty = jnp.zeros((NSRC, LAGS, CHANNELS), jnp.float32)
    (linear, phase_re, phase_im), _ = lax.scan(one_window, (empty, empty, empty), spectra)
    weighted = linear / WINDOWS * ((phase_re * phase_re + phase_im * phase_im) / (WINDOWS * WINDOWS))
    forward = forward_table(BINS, 0, LAGS)
    spectrum = jnp.einsum('kt,stc->skc', forward, weighted, precision=highest)
    spec_re = spectrum[:, :BINS]
    spec_im = spectrum[:, BINS:]
    scaling = WINDOWS ** 1.5 / math.sqrt(CHANNELS)
    group_size = math.gcd(NSLOW, 8)
    groups = jnp.arange(NSLOW, dtype=jnp.int32).reshape(NSLOW // group_size, group_size)

    def one_group(slowness):
        return slant_block(spec_re, spec_im, slowness, offsets, BINS)
    pieces = lax.map(one_group, groups)
    return pieces.reshape(NSLOW, NSRC, 2, BINS) * scaling
```

```python
import functools
import math

import jax
import jax.numpy as jnp
import numpy as np
from jax import lax
from jax.experimental import pallas as pl
from jax.experimental.pallas import tpu as pltpu
from jax.sharding import PartitionSpec as P

BINS = 256
LAGS = 512
NSLOW = 128
NSRC = 2
PERIOD = 4096
LANES = 128
FAST = 8
SLOW = NSLOW // FAST
GROUP = 16
GROUPS = BINS // GROUP
BOTH = ("days", "chan")
NT = (((1,), (1,)), ((), ()))


def inverse_table():
    lag = np.arange(LAGS)[:, None]
    freq = np.arange(BINS)[None, :]
    theta = (lag * freq % LAGS) * (2.0 * math.pi / LAGS)
    cosine, sine = np.cos(theta), np.sin(theta)
    table = np.block([[cosine, -sine], [sine, cosine]]) / math.sqrt(BINS)
    return table.astype(np.float32).astype(jnp.bfloat16)


def forward_tables(scale):
    freq = np.arange(BINS)[:, None]
    lag = np.arange(LAGS)[None, :]
    theta = (freq * lag % LAGS) * (2.0 * math.pi / LAGS)
    table = np.concatenate([np.cos(theta), -np.sin(theta)], 0) * (scale / math.sqrt(LAGS))
    high = table.astype(np.float32).astype(jnp.bfloat16)
    low = (table - high.astype(np.float64)).astype(np.float32).astype(jnp.bfloat16)
    return high, low


def columns_kernel(sources, spectra, sent):
    windows = spectra.shape[0]
    parts = 2 * BINS // LANES
    block = windows * parts
    peers = sent.shape[0] // block
    row = lax.broadcasted_iota(jnp.int32, (NSRC * block, LANES), 0)
    lane = lax.broadcasted_iota(jnp.int32, (NSRC * block, LANES), 1)
    column = jnp.where(row < block, lax.rem(sources[0], LANES), lax.rem(sources[1], LANES))
    hit = jnp.where(lane == column, row % block, -1)
    total = jnp.zeros((NSRC * block, LANES), jnp.float32)
    for place in range(block):
        window, part = divmod(place, parts)
        chosen = jnp.where(hit == place, 1.0, 0.0).astype(jnp.bfloat16)
        piece = spectra[window, part * LANES : (part + 1) * LANES, :]
        total += lax.dot_general(chosen, piece, NT, preferred_element_type=jnp.float32)
    rounded = total.astype(jnp.bfloat16)
    half = peers // NSRC
    for peer in range(peers):
        source = peer // half
        sent[peer * block : (peer + 1) * block, :] = rounded[source * block : (source + 1) * block]


def unit_circle(phase):
    quarter = PERIOD // 4
    turn = (phase + quarter // 2) // quarter
    angle = (phase - turn * quarter).astype(jnp.float32) * (2.0 * math.pi / PERIOD)
    square = angle * angle
    cosine = 1.0 + square * (-1 / 2 + square * (1 / 24 + square * (-1 / 720 + square * (1 / 40320))))
    sine = angle * (1.0 + square * (-1 / 6 + square * (1 / 120 + square * (-1 / 5040 + square * (1 / 362880)))))
    odd = (turn & 1) == 1
    real = jnp.where(odd, sine, cosine)
    imag = jnp.where(odd, cosine, sine)
    real = jnp.where(((turn + 1) & 2) == 2, -real, real)
    imag = jnp.where((turn & 2) == 2, -imag, imag)
    return real, imag


def times(left, right):
    return left[0] * right[0] - left[1] * right[1], left[0] * right[1] + left[1] * right[0]


def main_kernel(
    sources, received, own, other, offsets, inverse, high, low,
    sent,
    picked, cross, analytic, stack, steep, turned, rotor, arrived,
):
    windows = own.shape[0]
    parts = 2 * BINS // LANES
    block = windows * parts
    half = received.shape[0] // block // NSRC
    day = lax.axis_index("days")
    holder = sources[day] // LANES
    copies = []
    for side, from_day in enumerate((day, 1 - day)):
        start = pl.multiple_of((from_day * half + holder) * block, block)
        copies.append(
            pltpu.make_async_copy(
                received.at[pl.ds(start, block)], picked.at[pl.ds(side * block, block)], arrived.at[side]
            )
        )
    for copy in copies:
        copy.start()

    freq = lax.broadcasted_iota(jnp.int32, (BINS, LANES), 0)
    phase = freq * offsets[...] & (PERIOD - 1)
    base = unit_circle(phase)
    rotor[0], rotor[1] = base
    step = base
    for _ in range(int(math.log2(FAST))):
        step = times(step, step)
    value = (jnp.ones((BINS, LANES), jnp.float32), jnp.zeros((BINS, LANES), jnp.float32))
    for slow in range(SLOW):
        for part in range(2):
            rounded = value[part].astype(jnp.bfloat16)
            for group in range(GROUPS):
                steep[group, (slow + group) % SLOW, :, part * LANES : (part + 1) * LANES] = rounded[
                    group * GROUP : (group + 1) * GROUP
                ]
        if slow < SLOW - 1:
            value = times(value, step)

    for copy in copies:
        copy.wait()
    columns = jnp.transpose(picked[...].astype(jnp.float32))
    for window in range(2 * windows):
        taken = own if window < windows else other
        inner = window % windows
        for part in range(parts // 2):
            rows = slice(part * LANES, (part + 1) * LANES)
            far = slice(BINS + part * LANES, BINS + (part + 1) * LANES)
            place = window * parts + part
            real_s = jnp.broadcast_to(columns[:, place : place + 1], (LANES, LANES))
            place += parts // 2
            imag_s = jnp.broadcast_to(columns[:, place : place + 1], (LANES, LANES))
            real_x = taken[inner, rows, :].astype(jnp.float32)
            imag_x = taken[inner, far, :].astype(jnp.float32)
            lanes = slice(window * LANES, (window + 1) * LANES)
            cross[rows, lanes] = (real_s * real_x + imag_s * imag_x).astype(jnp.bfloat16)
            cross[far, lanes] = (real_s * imag_x - imag_s * real_x).astype(jnp.bfloat16)

    for pair in range(windows):
        analytic[pair] = jnp.dot(
            inverse[...], cross[:, pair * 2 * LANES : (pair + 1) * 2 * LANES], preferred_element_type=jnp.float32
        )
    chunk = 32
    for first in range(0, LAGS, chunk):
        linear = phase_re = phase_im = None
        for window in range(2 * windows):
            lanes = slice(window % 2 * LANES, (window % 2 + 1) * LANES)
            corr = analytic[window // 2, first : first + chunk, lanes]
            hilb = analytic[window // 2, LAGS + first : LAGS + first + chunk, lanes]
            weight = lax.rsqrt(jnp.maximum(corr * corr + hilb * hilb, 0.25))
            if window == 0:
                linear, phase_re, phase_im = corr, corr * weight, hilb * weight
            else:
                linear += corr
                phase_re += corr * weight
                phase_im += hilb * weight
        weighted = linear * (phase_re * phase_re + phase_im * phase_im)
        large = weighted.astype(jnp.bfloat16)
        stack[first : first + chunk, :LANES] = large
        stack[first : first + chunk, LANES:] = (weighted - large.astype(jnp.float32)).astype(jnp.bfloat16)

    wide = jnp.dot(high[...], stack[...], preferred_element_type=jnp.float32)
    spectrum = (
        wide[:, :LANES]
        + wide[:, LANES:]
        + jnp.dot(low[...], stack[:, :LANES], preferred_element_type=jnp.float32)
    )
    value = (spectrum[:BINS], spectrum[BINS:])
    base = (rotor[0], rotor[1])
    for fast in range(FAST):
        real = value[0].astype(jnp.bfloat16).reshape(GROUPS, GROUP, LANES)
        imag = value[1].astype(jnp.bfloat16).reshape(GROUPS, GROUP, LANES)
        turned[:, 2 * fast, :, :LANES] = real
        turned[:, 2 * fast, :, LANES:] = -imag
        turned[:, 2 * fast + 1, :, :LANES] = imag
        turned[:, 2 * fast + 1, :, LANES:] = real
        if fast < FAST - 1:
            value = times(value, base)

    side = 2 * FAST * GROUP
    row = lax.broadcasted_iota(jnp.int32, (side, SLOW * GROUP), 0)
    lane = lax.broadcasted_iota(jnp.int32, (side, SLOW * GROUP), 1)
    same = row % GROUP == lane % GROUP
    gather_row = lax.broadcasted_iota(jnp.int32, (2 * FAST, side), 0)
    gather_lane = lax.broadcasted_iota(jnp.int32, (2 * FAST, side), 1)
    gather = jnp.where(gather_lane // GROUP == gather_row, 1.0, 0.0).astype(jnp.bfloat16)
    kept = []
    for group in range(GROUPS):
        product = lax.dot_general(
            turned[group].reshape(side, 2 * LANES),
            steep[group].reshape(SLOW * GROUP, 2 * LANES),
            NT,
            preferred_element_type=jnp.float32,
        )
        diagonal = jnp.where(same, product, 0.0).astype(jnp.bfloat16)
        kept.append(jnp.dot(gather, diagonal, preferred_element_type=jnp.float32))

    spot = lax.broadcasted_iota(jnp.int32, (2 * FAST, BINS), 1) // GROUP
    low_rows = lax.broadcasted_iota(jnp.int32, (8, LANES), 0) < 4
    for slow in range(SLOW):
        joined = kept[-slow % GROUPS]
        for place in range(1, GROUPS):
            joined = jnp.where(spot == place, kept[(place - slow) % GROUPS], joined)
        if slow:
            joined = pltpu.roll(joined, BINS - slow * GROUP, 1)
        for pair in range(2):
            left = joined[8 * pair : 8 * pair + 8, :LANES]
            right = joined[8 * pair : 8 * pair + 8, LANES:]
            first = jnp.where(low_rows, left, pltpu.roll(right, 4, 0))
            second = jnp.where(low_rows, pltpu.roll(left, 4, 0), right)
            tile = jnp.concatenate([first, second], 0).astype(jnp.bfloat16)
            for day_side in range(2):
                start = (day_side * half + slow * (FAST // 2) + 2 * pair) * 8
                sent[start : start + 16, :] = tile


def sum_kernel(received, out):
    rows = received.shape[0] // NSRC
    for source in range(NSRC):
        terms = received[source * rows : (source + 1) * rows, :].astype(jnp.float32)
        total = jnp.sum(terms.reshape(rows // 8, 8, LANES), 0)
        for row in range(8):
            upper, slow, part = row // 4, row // 2 % 2, row % 2
            out[slow, source, part, upper * LANES : (upper + 1) * LANES] = total[row]


def shards(spectra, sources, offsets):
    windows = spectra.shape[0]
    width = spectra.shape[2]
    peers = lax.axis_size("days") * lax.axis_size("chan")
    all_windows = windows * lax.axis_size("days")
    channels = width * lax.axis_size("chan")
    scale = all_windows**1.5 / math.sqrt(channels) / all_windows**3
    high, low = forward_tables(scale)
    vmem = pl.BlockSpec(memory_space=pltpu.VMEM)
    smem = pl.BlockSpec(memory_space=pltpu.SMEM)
    anywhere = pl.BlockSpec(memory_space=pl.ANY)
    block = windows * 2 * BINS // LANES

    other = lax.ppermute(spectra, "days", [(0, 1), (1, 0)])
    candidates = pl.pallas_call(
        columns_kernel,
        out_shape=jax.ShapeDtypeStruct((peers * block, LANES), jnp.bfloat16),
        in_specs=[smem, vmem],
        out_specs=vmem,
        name="columns",
        compiler_params=pltpu.CompilerParams(vmem_limit_bytes=8 << 20),
    )(sources, spectra)
    received = lax.all_to_all(candidates.reshape(peers, block, LANES), BOTH, 0, 0, tiled=True)
    received = received.reshape(peers * block, LANES)
    terms = pl.pallas_call(
        main_kernel,
        out_shape=jax.ShapeDtypeStruct((peers * 8, LANES), jnp.bfloat16),
        in_specs=[smem, anywhere] + [vmem] * 6,
        out_specs=vmem,
        scratch_shapes=[
            pltpu.VMEM((2 * block, LANES), jnp.bfloat16),
            pltpu.VMEM((2 * BINS, all_windows * LANES), jnp.bfloat16),
            pltpu.VMEM((windows, 2 * LAGS, 2 * LANES), jnp.float32),
            pltpu.VMEM((LAGS, 2 * LANES), jnp.bfloat16),
            pltpu.VMEM((GROUPS, SLOW, GROUP, 2 * LANES), jnp.bfloat16),
            pltpu.VMEM((GROUPS, 2 * FAST, GROUP, 2 * LANES), jnp.bfloat16),
            pltpu.VMEM((2, BINS, LANES), jnp.float32),
            pltpu.SemaphoreType.DMA((2,)),
        ],
        name="stack_and_slant",
        compiler_params=pltpu.CompilerParams(vmem_limit_bytes=32 << 20),
    )(sources, received, spectra, other, offsets.reshape(1, width), inverse_table(), high, low)
    partial = lax.all_to_all(terms.reshape(peers, 8, LANES), BOTH, 0, 0, tiled=True)
    return pl.pallas_call(
        sum_kernel,
        out_shape=jax.ShapeDtypeStruct((NSLOW // lax.axis_size("chan"), NSRC, 2, BINS), jnp.float32),
        in_specs=[vmem],
        out_specs=vmem,
        name="sum",
        compiler_params=pltpu.CompilerParams(vmem_limit_bytes=8 << 20),
    )(partial.reshape(peers * 8, LANES))


def solution(mesh):
    placed = (P("days", None, "chan"), P(), P("chan"))
    return jax.shard_map(
        shards, mesh=mesh, in_specs=placed, out_specs=P("chan", None, None, None), check_vma=False
    )
```

```python
import math

import jax
import jax.numpy as jnp
import numpy as np
from jax import lax
from jax.experimental import pallas as pl
from jax.experimental.pallas import tpu as pltpu
from jax.sharding import PartitionSpec as P

BINS = 256
LAGS = 512
NSLOW = 128
NSRC = 2
PERIOD = 4096
LANES = 128
FAST = 8
SLOW = NSLOW // FAST
GROUP = 16
GROUPS = BINS // GROUP
BOTH = ("days", "chan")
NT = (((1,), (1,)), ((), ()))


def inverse_table():
    lag = np.arange(LAGS)[:, None]
    freq = np.arange(BINS)[None, :]
    theta = (lag * freq % LAGS) * (2.0 * math.pi / LAGS)
    cosine, sine = np.cos(theta), np.sin(theta)
    table = np.block([[cosine, -sine], [sine, cosine]]) / math.sqrt(BINS)
    return table.astype(np.float32).astype(jnp.bfloat16)


def forward_table(scale):
    freq = np.arange(BINS)[:, None]
    lag = np.arange(LAGS)[None, :]
    theta = (freq * lag % LAGS) * (2.0 * math.pi / LAGS)
    table = np.concatenate([np.cos(theta), -np.sin(theta)], 0) * (scale / math.sqrt(LAGS))
    high = table.astype(np.float32).astype(jnp.bfloat16)
    low = (table - high.astype(np.float64)).astype(np.float32).astype(jnp.bfloat16)
    return np.concatenate([high, low], 0)


def unit_circle(phase):
    quarter = PERIOD // 4
    turn = (phase + quarter // 2) >> 10
    angle = (phase - turn * quarter).astype(jnp.float32) * (2.0 * math.pi / PERIOD)
    square = angle * angle
    cosine = 1.0 + square * (-1 / 2 + square * (1 / 24 + square * (-1 / 720 + square * (1 / 40320))))
    sine = angle * (1.0 + square * (-1 / 6 + square * (1 / 120 + square * (-1 / 5040 + square * (1 / 362880)))))
    odd = (turn & 1) == 1
    real = jnp.where(odd, sine, cosine)
    imag = jnp.where(odd, cosine, sine)
    real = jnp.where(((turn + 1) & 2) == 2, -real, real)
    imag = jnp.where((turn & 2) == 2, -imag, imag)
    return real, imag


def times(left, right):
    return left[0] * right[0] - left[1] * right[1], left[0] * right[1] + left[1] * right[0]


def front_kernel(
    sources, offsets, spectra, inverse_far, forward_far,
    sent, steep, rotor, held, inverse, forward,
    places, spots, arrived,
):
    windows = spectra.shape[0]
    parts = 2 * BINS // LANES
    block = windows * parts
    peers = sent.shape[0] // block
    pairs = ((offsets, spots), (sources, places), (spectra, held), (inverse_far, inverse), (forward_far, forward))
    copies = [pltpu.make_async_copy(*pair, arrived.at[place]) for place, pair in enumerate(pairs)]
    for copy in copies:
        copy.start()

    copies[0].wait()
    freq = lax.broadcasted_iota(jnp.int32, (BINS, LANES), 0)
    base = unit_circle(freq * spots[...] & (PERIOD - 1))
    rotor[0], rotor[1] = base
    step = base
    for _ in range(int(math.log2(FAST))):
        step = times(step, step)
    value = (jnp.ones((BINS, LANES), jnp.float32), jnp.zeros((BINS, LANES), jnp.float32))
    for slow in range(SLOW):
        for part in range(2):
            rounded = value[part].astype(jnp.bfloat16)
            for group in range(GROUPS):
                steep[group, (slow + group) % SLOW, :, part * LANES : (part + 1) * LANES] = rounded[
                    group * GROUP : (group + 1) * GROUP
                ]
        if slow < SLOW - 1:
            value = times(value, step)

    copies[1].wait()
    row = lax.broadcasted_iota(jnp.int32, (NSRC * block, LANES), 0)
    lane = lax.broadcasted_iota(jnp.int32, (NSRC * block, LANES), 1)
    column = jnp.where(row < block, places[:, 0:1], places[:, 1:2]) - lax.axis_index("chan") * LANES
    hit = jnp.where(lane == column, row & (block - 1), -1)
    total = jnp.zeros((NSRC * block, LANES), jnp.float32)
    copies[2].wait()
    for place in range(block):
        window, part = divmod(place, parts)
        chosen = jnp.where(hit == place, 1.0, 0.0).astype(jnp.bfloat16)
        piece = held[window, part * LANES : (part + 1) * LANES, :]
        total += lax.dot_general(chosen, piece, NT, preferred_element_type=jnp.float32)
    rounded = total.astype(jnp.bfloat16)
    half = peers // NSRC
    for peer in range(peers):
        source = peer // half
        sent[peer * block : (peer + 1) * block, :] = rounded[source * block : (source + 1) * block]
    copies[3].wait()
    copies[4].wait()


def main_kernel(
    received, own, other, steep, rotor, inverse, forward,
    sent,
    cross, analytic, stack, turned,
):
    windows = own.shape[0]
    parts = 2 * BINS // LANES
    block = windows * parts
    half = received.shape[0] // block // NSRC
    day = lax.axis_index("days")
    picked = []
    for from_day in (day, 1 - day):
        total = None
        for peer in range(half):
            start = pl.multiple_of((from_day * half + peer) * block, block)
            term = received[pl.ds(start, block), :]
            total = term if peer == 0 else total + term
        picked.append(total.astype(jnp.float32))
    columns = jnp.transpose(jnp.concatenate(picked, 0))
    for window in range(2 * windows):
        taken = own if window < windows else other
        inner = window % windows
        for part in range(parts // 2):
            rows = slice(part * LANES, (part + 1) * LANES)
            far = slice(BINS + part * LANES, BINS + (part + 1) * LANES)
            place = window * parts + part
            real_s = jnp.broadcast_to(columns[:, place : place + 1], (LANES, LANES))
            place += parts // 2
            imag_s = jnp.broadcast_to(columns[:, place : place + 1], (LANES, LANES))
            real_x = taken[inner, rows, :].astype(jnp.float32)
            imag_x = taken[inner, far, :].astype(jnp.float32)
            lanes = slice(window * LANES, (window + 1) * LANES)
            cross[rows, lanes] = (real_s * real_x + imag_s * imag_x).astype(jnp.bfloat16)
            cross[far, lanes] = (real_s * imag_x - imag_s * real_x).astype(jnp.bfloat16)

    for pair in range(windows):
        analytic[pair] = jnp.dot(
            inverse[...], cross[:, pair * 2 * LANES : (pair + 1) * 2 * LANES], preferred_element_type=jnp.float32
        )
    chunk = 32
    for first in range(0, LAGS, chunk):
        linear = phase_re = phase_im = None
        for window in range(2 * windows):
            lanes = slice(window % 2 * LANES, (window % 2 + 1) * LANES)
            corr = analytic[window // 2, first : first + chunk, lanes]
            hilb = analytic[window // 2, LAGS + first : LAGS + first + chunk, lanes]
            weight = lax.rsqrt(jnp.maximum(corr * corr + hilb * hilb, 0.25))
            if window == 0:
                linear, phase_re, phase_im = corr, corr * weight, hilb * weight
            else:
                linear += corr
                phase_re += corr * weight
                phase_im += hilb * weight
        weighted = linear * (phase_re * phase_re + phase_im * phase_im)
        large = weighted.astype(jnp.bfloat16)
        stack[first : first + chunk, :LANES] = large
        stack[first : first + chunk, LANES:] = (weighted - large.astype(jnp.float32)).astype(jnp.bfloat16)

    wide = jnp.dot(forward[: 2 * BINS, :], stack[...], preferred_element_type=jnp.float32)
    spectrum = (
        wide[:, :LANES]
        + wide[:, LANES:]
        + jnp.dot(forward[2 * BINS :, :], stack[:, :LANES], preferred_element_type=jnp.float32)
    )
    value = (spectrum[:BINS], spectrum[BINS:])
    base = (rotor[0], rotor[1])
    for fast in range(FAST):
        real = value[0].astype(jnp.bfloat16).reshape(GROUPS, GROUP, LANES)
        imag = value[1].astype(jnp.bfloat16).reshape(GROUPS, GROUP, LANES)
        turned[:, 2 * fast, :, :LANES] = real
        turned[:, 2 * fast, :, LANES:] = -imag
        turned[:, 2 * fast + 1, :, :LANES] = imag
        turned[:, 2 * fast + 1, :, LANES:] = real
        if fast < FAST - 1:
            value = times(value, base)

    side = 2 * FAST * GROUP
    row = lax.broadcasted_iota(jnp.int32, (side, SLOW * GROUP), 0)
    lane = lax.broadcasted_iota(jnp.int32, (side, SLOW * GROUP), 1)
    same = row % GROUP == lane % GROUP
    gather_row = lax.broadcasted_iota(jnp.int32, (2 * FAST, side), 0)
    gather_lane = lax.broadcasted_iota(jnp.int32, (2 * FAST, side), 1)
    gather = jnp.where(gather_lane // GROUP == gather_row, 1.0, 0.0).astype(jnp.bfloat16)
    kept = []
    for group in range(GROUPS):
        product = lax.dot_general(
            turned[group].reshape(side, 2 * LANES),
            steep[group].reshape(SLOW * GROUP, 2 * LANES),
            NT,
            preferred_element_type=jnp.float32,
        )
        diagonal = jnp.where(same, product, 0.0).astype(jnp.bfloat16)
        kept.append(jnp.dot(gather, diagonal, preferred_element_type=jnp.float32))

    spot = lax.broadcasted_iota(jnp.int32, (2 * FAST, BINS), 1) // GROUP
    low_rows = lax.broadcasted_iota(jnp.int32, (8, LANES), 0) < 4
    for slow in range(SLOW):
        joined = kept[-slow % GROUPS]
        for place in range(1, GROUPS):
            joined = jnp.where(spot == place, kept[(place - slow) % GROUPS], joined)
        if slow:
            joined = pltpu.roll(joined, BINS - slow * GROUP, 1)
        for pair in range(2):
            left = joined[8 * pair : 8 * pair + 8, :LANES]
            right = joined[8 * pair : 8 * pair + 8, LANES:]
            first = jnp.where(low_rows, left, pltpu.roll(right, 4, 0))
            second = jnp.where(low_rows, pltpu.roll(left, 4, 0), right)
            tile = jnp.concatenate([first, second], 0).astype(jnp.bfloat16)
            for day_side in range(2):
                start = (day_side * half + slow * (FAST // 2) + 2 * pair) * 8
                sent[start : start + 16, :] = tile


def sum_kernel(received, out):
    rows = received.shape[0] // NSRC
    for source in range(NSRC):
        terms = received[source * rows : (source + 1) * rows, :].astype(jnp.float32)
        total = jnp.sum(terms.reshape(rows // 8, 8, LANES), 0)
        for row in range(8):
            upper, slow, part = row // 4, row // 2 % 2, row % 2
            out[slow, source, part, upper * LANES : (upper + 1) * LANES] = total[row]


def in_hbm(array):
    return pltpu.with_memory_space_constraint(array, pltpu.HBM)


def shards(spectra, sources, offsets):
    windows = spectra.shape[0]
    width = spectra.shape[2]
    peers = lax.axis_size("days") * lax.axis_size("chan")
    all_windows = windows * lax.axis_size("days")
    channels = width * lax.axis_size("chan")
    scale = all_windows**1.5 / math.sqrt(channels) / all_windows**3
    forward = forward_table(scale)
    vmem = pl.BlockSpec(memory_space=pltpu.VMEM)
    far = pl.BlockSpec(memory_space=pltpu.HBM)
    block = windows * 2 * BINS // LANES

    other = lax.ppermute(spectra, "days", [(0, 1), (1, 0)])
    inverse = jnp.asarray(inverse_table())
    forward = jnp.asarray(forward)
    candidates, steep, rotor, own, inverse, forward = pl.pallas_call(
        front_kernel,
        out_shape=(
            jax.ShapeDtypeStruct((peers * block, LANES), jnp.bfloat16),
            jax.ShapeDtypeStruct((GROUPS, SLOW, GROUP, 2 * LANES), jnp.bfloat16),
            jax.ShapeDtypeStruct((2, BINS, LANES), jnp.float32),
            jax.ShapeDtypeStruct(spectra.shape, jnp.bfloat16),
            jax.ShapeDtypeStruct(inverse.shape, jnp.bfloat16),
            jax.ShapeDtypeStruct(forward.shape, jnp.bfloat16),
        ),
        in_specs=[far] * 5,
        out_specs=(vmem,) * 6,
        scratch_shapes=[
            pltpu.VMEM((1, NSRC), jnp.int32),
            pltpu.VMEM((1, width), jnp.int32),
            pltpu.SemaphoreType.DMA((5,)),
        ],
        name="front",
        compiler_params=pltpu.CompilerParams(vmem_limit_bytes=8 << 20),
    )(
        in_hbm(sources.reshape(1, NSRC)),
        in_hbm(offsets.reshape(1, width)),
        in_hbm(spectra),
        in_hbm(inverse),
        in_hbm(forward),
    )
    received = lax.all_to_all(candidates.reshape(peers, block, LANES), BOTH, 0, 0, tiled=True)
    received = received.reshape(peers * block, LANES)
    terms = pl.pallas_call(
        main_kernel,
        out_shape=jax.ShapeDtypeStruct((peers * 8, LANES), jnp.bfloat16),
        in_specs=[vmem] * 7,
        out_specs=vmem,
        scratch_shapes=[
            pltpu.VMEM((2 * BINS, all_windows * LANES), jnp.bfloat16),
            pltpu.VMEM((windows, 2 * LAGS, 2 * LANES), jnp.float32),
            pltpu.VMEM((LAGS, 2 * LANES), jnp.bfloat16),
            pltpu.VMEM((GROUPS, 2 * FAST, GROUP, 2 * LANES), jnp.bfloat16),
        ],
        name="stack_and_slant",
        compiler_params=pltpu.CompilerParams(vmem_limit_bytes=24 << 20),
    )(received, own, other, steep, rotor, inverse, forward)
    partial = lax.all_to_all(terms.reshape(peers, 8, LANES), BOTH, 0, 0, tiled=True)
    return pl.pallas_call(
        sum_kernel,
        out_shape=jax.ShapeDtypeStruct((NSLOW // lax.axis_size("chan"), NSRC, 2, BINS), jnp.float32),
        in_specs=[vmem],
        out_specs=vmem,
        name="sum",
        compiler_params=pltpu.CompilerParams(vmem_limit_bytes=8 << 20),
    )(partial.reshape(peers * 8, LANES))


def solution(mesh):
    placed = (P("days", None, "chan"), P(), P("chan"))
    return jax.shard_map(
        shards, mesh=mesh, in_specs=placed, out_specs=P("chan", None, None, None), check_vma=False
    )
```

```python
import math

import jax
import jax.numpy as jnp
import numpy as np
from jax import lax
from jax.experimental import pallas as pl
from jax.experimental.pallas import tpu as pltpu
from jax.sharding import PartitionSpec as P

BINS = 256
LAGS = 512
NSLOW = 128
NSRC = 2
PERIOD = 4096
LANES = 128
FAST = 8
SLOW = NSLOW // FAST
GROUP = 8
GROUPS = BINS // GROUP
BOTH = ("days", "chan")
NT = (((1,), (1,)), ((), ()))


def inverse_table():
    lag = np.arange(LAGS)[:, None]
    freq = np.arange(BINS)[None, :]
    theta = (lag * freq % LAGS) * (2.0 * math.pi / LAGS)
    cosine, sine = np.cos(theta), np.sin(theta)
    table = np.block([[cosine, -sine], [sine, cosine]]) / math.sqrt(BINS)
    return table.astype(np.float32).astype(jnp.bfloat16)


def forward_table(scale):
    freq = np.arange(BINS)[:, None]
    lag = np.arange(LAGS)[None, :]
    theta = (freq * lag % LAGS) * (2.0 * math.pi / LAGS)
    table = np.concatenate([np.cos(theta), -np.sin(theta)], 0) * (scale / math.sqrt(LAGS))
    high = table.astype(np.float32).astype(jnp.bfloat16)
    low = (table - high.astype(np.float64)).astype(np.float32).astype(jnp.bfloat16)
    return np.concatenate([high, low], 0)


def unit_circle(phase):
    quarter = PERIOD // 4
    turn = (phase + quarter // 2) >> 10
    angle = (phase - turn * quarter).astype(jnp.float32) * (2.0 * math.pi / PERIOD)
    square = angle * angle
    cosine = 1.0 + square * (-1 / 2 + square * (1 / 24 + square * (-1 / 720 + square * (1 / 40320))))
    sine = angle * (1.0 + square * (-1 / 6 + square * (1 / 120 + square * (-1 / 5040 + square * (1 / 362880)))))
    odd = (turn & 1) == 1
    real = jnp.where(odd, sine, cosine)
    imag = jnp.where(odd, cosine, sine)
    real = jnp.where(((turn + 1) & 2) == 2, -real, real)
    imag = jnp.where((turn & 2) == 2, -imag, imag)
    return real, imag


def times(left, right):
    return left[0] * right[0] - left[1] * right[1], left[0] * right[1] + left[1] * right[0]


def front_kernel(
    sources, offsets, spectra, inverse_far, forward_far,
    sent, steep, rotor, held, inverse, forward,
    places, spots, arrived,
):
    windows = spectra.shape[0]
    parts = 2 * BINS // LANES
    block = windows * parts
    peers = sent.shape[0] // block
    pairs = ((offsets, spots), (sources, places), (spectra, held), (inverse_far, inverse), (forward_far, forward))
    copies = [pltpu.make_async_copy(*pair, arrived.at[place]) for place, pair in enumerate(pairs)]
    for copy in copies:
        copy.start()

    copies[0].wait()
    freq = lax.broadcasted_iota(jnp.int32, (BINS, LANES), 0)
    rotor[0], rotor[1] = unit_circle(freq * spots[...] & (PERIOD - 1))
    across = jnp.transpose(jnp.broadcast_to(spots[...].astype(jnp.float32), (LANES, LANES))).astype(jnp.int32)
    lane = lax.broadcasted_iota(jnp.int32, (LANES, LANES), 1)
    turn = across * (lane // GROUP * FAST)
    value = unit_circle(turn * (lane & (GROUP - 1)) & (PERIOD - 1))
    step = unit_circle(turn * GROUP & (PERIOD - 1))
    for group in range(GROUPS):
        steep[group, :LANES, :] = value[0].astype(jnp.bfloat16)
        steep[group, LANES:, :] = value[1].astype(jnp.bfloat16)
        if group < GROUPS - 1:
            value = times(value, step)

    copies[1].wait()
    row = lax.broadcasted_iota(jnp.int32, (NSRC * block, LANES), 0)
    lane = lax.broadcasted_iota(jnp.int32, (NSRC * block, LANES), 1)
    column = jnp.where(row < block, places[:, 0:1], places[:, 1:2]) - lax.axis_index("chan") * LANES
    hit = jnp.where(lane == column, row & (block - 1), -1)
    total = jnp.zeros((NSRC * block, LANES), jnp.float32)
    copies[2].wait()
    for place in range(block):
        window, part = divmod(place, parts)
        chosen = jnp.where(hit == place, 1.0, 0.0).astype(jnp.bfloat16)
        piece = held[window, part * LANES : (part + 1) * LANES, :]
        total += lax.dot_general(chosen, piece, NT, preferred_element_type=jnp.float32)
    rounded = total.astype(jnp.bfloat16)
    half = peers // NSRC
    for peer in range(peers):
        source = peer // half
        sent[peer * block : (peer + 1) * block, :] = rounded[source * block : (source + 1) * block]
    copies[3].wait()
    copies[4].wait()


def main_kernel(
    received, own, other, steep, rotor, inverse, forward,
    sent,
    cross, analytic, stack, turned, product,
):
    windows = own.shape[0]
    parts = 2 * BINS // LANES
    block = windows * parts
    half = received.shape[0] // block // NSRC
    day = lax.axis_index("days")
    picked = []
    for from_day in (day, 1 - day):
        total = None
        for peer in range(half):
            start = pl.multiple_of((from_day * half + peer) * block, block)
            term = received[pl.ds(start, block), :]
            total = term if peer == 0 else total + term
        picked.append(total.astype(jnp.float32))
    columns = jnp.transpose(jnp.concatenate(picked, 0))
    for window in range(2 * windows):
        taken = own if window < windows else other
        inner = window % windows
        for part in range(parts // 2):
            rows = slice(part * LANES, (part + 1) * LANES)
            far = slice(BINS + part * LANES, BINS + (part + 1) * LANES)
            place = window * parts + part
            real_s = jnp.broadcast_to(columns[:, place : place + 1], (LANES, LANES))
            place += parts // 2
            imag_s = jnp.broadcast_to(columns[:, place : place + 1], (LANES, LANES))
            real_x = taken[inner, rows, :].astype(jnp.float32)
            imag_x = taken[inner, far, :].astype(jnp.float32)
            lanes = slice(window * LANES, (window + 1) * LANES)
            cross[rows, lanes] = (real_s * real_x + imag_s * imag_x).astype(jnp.bfloat16)
            cross[far, lanes] = (real_s * imag_x - imag_s * real_x).astype(jnp.bfloat16)

    for pair in range(windows):
        analytic[pair] = jnp.dot(
            inverse[...], cross[:, pair * 2 * LANES : (pair + 1) * 2 * LANES], preferred_element_type=jnp.float32
        )
    chunk = 32
    for first in range(0, LAGS, chunk):
        linear = phase_re = phase_im = None
        for window in range(2 * windows):
            lanes = slice(window % 2 * LANES, (window % 2 + 1) * LANES)
            corr = analytic[window // 2, first : first + chunk, lanes]
            hilb = analytic[window // 2, LAGS + first : LAGS + first + chunk, lanes]
            weight = lax.rsqrt(jnp.maximum(corr * corr + hilb * hilb, 0.25))
            if window == 0:
                linear, phase_re, phase_im = corr, corr * weight, hilb * weight
            else:
                linear += corr
                phase_re += corr * weight
                phase_im += hilb * weight
        weighted = linear * (phase_re * phase_re + phase_im * phase_im)
        large = weighted.astype(jnp.bfloat16)
        stack[first : first + chunk, :LANES] = large
        stack[first : first + chunk, LANES:] = (weighted - large.astype(jnp.float32)).astype(jnp.bfloat16)

    wide = jnp.dot(forward[: 2 * BINS, :], stack[...], preferred_element_type=jnp.float32)
    spectrum = (
        wide[:, :LANES]
        + wide[:, LANES:]
        + jnp.dot(forward[2 * BINS :, :], stack[:, :LANES], preferred_element_type=jnp.float32)
    )
    value = (spectrum[:BINS], spectrum[BINS:])
    base = (rotor[0], rotor[1])
    for fast in range(FAST):
        real = value[0].reshape(GROUPS, GROUP, LANES)
        imag = value[1].reshape(GROUPS, GROUP, LANES)
        turned[:, fast, :, :LANES] = jnp.concatenate([real, imag], 1).astype(jnp.bfloat16)
        turned[:, fast, :, LANES:] = jnp.concatenate([-imag, real], 1).astype(jnp.bfloat16)
        if fast < FAST - 1:
            value = times(value, base)

    side = 2 * FAST * GROUP
    bin_lane = lax.broadcasted_iota(jnp.int32, (8, LANES), 1) & (GROUP - 1)
    kept = []
    for group in range(GROUPS):
        product[group] = jnp.dot(
            turned[group].reshape(side, 2 * LANES), steep[group], preferred_element_type=jnp.float32
        )
        tiles = []
        for first in range(0, side, 8 * GROUP):
            tile = product[group, pl.ds(first, 8, stride=GROUP), :]
            for place in range(1, GROUP):
                tile = jnp.where(bin_lane == place, product[group, pl.ds(first + place, 8, stride=GROUP), :], tile)
            tiles.append(tile)
        kept.append(jnp.concatenate(tiles, 0))

    spot = lax.broadcasted_iota(jnp.int32, (2 * FAST, LANES), 1) // GROUP
    kept = [pltpu.roll(part, group % SLOW * GROUP, 1) if group % SLOW else part for group, part in enumerate(kept)]
    low_rows = lax.broadcasted_iota(jnp.int32, (8, LANES), 0) < 4
    for slow in range(SLOW):
        halves = []
        for first in (0, SLOW):
            joined = kept[first + -slow % SLOW]
            for place in range(1, SLOW):
                joined = jnp.where(spot == place, kept[first + (place - slow) % SLOW], joined)
            halves.append(pltpu.roll(joined, LANES - slow * GROUP, 1) if slow else joined)
        for pair in range(2):
            left = halves[0][8 * pair : 8 * pair + 8]
            right = halves[1][8 * pair : 8 * pair + 8]
            first = jnp.where(low_rows, left, pltpu.roll(right, 4, 0))
            second = jnp.where(low_rows, pltpu.roll(left, 4, 0), right)
            tile = jnp.concatenate([first, second], 0).astype(jnp.bfloat16)
            for day_side in range(2):
                start = (day_side * half + slow * (FAST // 2) + 2 * pair) * 8
                sent[start : start + 16, :] = tile


def sum_kernel(received, out):
    rows = received.shape[0] // NSRC
    for source in range(NSRC):
        terms = received[source * rows : (source + 1) * rows, :].astype(jnp.float32)
        total = jnp.sum(terms.reshape(rows // 8, 8, LANES), 0)
        for row in range(8):
            upper, slow, part = row // 4, row // 2 % 2, row % 2
            out[slow, source, part, upper * LANES : (upper + 1) * LANES] = total[row]


def in_hbm(array):
    return pltpu.with_memory_space_constraint(array, pltpu.HBM)


def shards(spectra, sources, offsets):
    windows = spectra.shape[0]
    width = spectra.shape[2]
    peers = lax.axis_size("days") * lax.axis_size("chan")
    all_windows = windows * lax.axis_size("days")
    channels = width * lax.axis_size("chan")
    scale = all_windows**1.5 / math.sqrt(channels) / all_windows**3
    forward = forward_table(scale)
    vmem = pl.BlockSpec(memory_space=pltpu.VMEM)
    far = pl.BlockSpec(memory_space=pltpu.HBM)
    block = windows * 2 * BINS // LANES

    other = lax.ppermute(spectra, "days", [(0, 1), (1, 0)])
    inverse = jnp.asarray(inverse_table())
    forward = jnp.asarray(forward)
    candidates, steep, rotor, own, inverse, forward = pl.pallas_call(
        front_kernel,
        out_shape=(
            jax.ShapeDtypeStruct((peers * block, LANES), jnp.bfloat16),
            jax.ShapeDtypeStruct((GROUPS, 2 * LANES, LANES), jnp.bfloat16),
            jax.ShapeDtypeStruct((2, BINS, LANES), jnp.float32),
            jax.ShapeDtypeStruct(spectra.shape, jnp.bfloat16),
            jax.ShapeDtypeStruct(inverse.shape, jnp.bfloat16),
            jax.ShapeDtypeStruct(forward.shape, jnp.bfloat16),
        ),
        in_specs=[far] * 5,
        out_specs=(vmem,) * 6,
        scratch_shapes=[
            pltpu.VMEM((1, NSRC), jnp.int32),
            pltpu.VMEM((1, width), jnp.int32),
            pltpu.SemaphoreType.DMA((5,)),
        ],
        name="front",
        compiler_params=pltpu.CompilerParams(vmem_limit_bytes=8 << 20),
    )(
        in_hbm(sources.reshape(1, NSRC)),
        in_hbm(offsets.reshape(1, width)),
        in_hbm(spectra),
        in_hbm(inverse),
        in_hbm(forward),
    )
    received = lax.all_to_all(candidates.reshape(peers, block, LANES), BOTH, 0, 0, tiled=True)
    received = received.reshape(peers * block, LANES)
    terms = pl.pallas_call(
        main_kernel,
        out_shape=jax.ShapeDtypeStruct((peers * 8, LANES), jnp.bfloat16),
        in_specs=[vmem] * 7,
        out_specs=vmem,
        scratch_shapes=[
            pltpu.VMEM((2 * BINS, all_windows * LANES), jnp.bfloat16),
            pltpu.VMEM((windows, 2 * LAGS, 2 * LANES), jnp.float32),
            pltpu.VMEM((LAGS, 2 * LANES), jnp.bfloat16),
            pltpu.VMEM((GROUPS, FAST, 2 * GROUP, 2 * LANES), jnp.bfloat16),
            pltpu.VMEM((GROUPS, 2 * FAST * GROUP, LANES), jnp.float32),
        ],
        name="stack_and_slant",
        compiler_params=pltpu.CompilerParams(vmem_limit_bytes=24 << 20),
    )(received, own, other, steep, rotor, inverse, forward)
    partial = lax.all_to_all(terms.reshape(peers, 8, LANES), BOTH, 0, 0, tiled=True)
    return pl.pallas_call(
        sum_kernel,
        out_shape=jax.ShapeDtypeStruct((NSLOW // lax.axis_size("chan"), NSRC, 2, BINS), jnp.float32),
        in_specs=[vmem],
        out_specs=vmem,
        name="sum",
        compiler_params=pltpu.CompilerParams(vmem_limit_bytes=8 << 20),
    )(partial.reshape(peers * 8, LANES))


def solution(mesh):
    placed = (P("days", None, "chan"), P(), P("chan"))
    return jax.shard_map(
        shards, mesh=mesh, in_specs=placed, out_specs=P("chan", None, None, None), check_vma=False
    )
```

```python
import functools
import math

import jax
import jax.numpy as jnp
import numpy as np
from jax import lax
from jax.experimental import pallas as pl
from jax.experimental.pallas import tpu as pltpu
from jax.sharding import PartitionSpec as P

BINS = 256
LAGS = 512
NSLOW = 128
NSRC = 2
PERIOD = 4096
LANES = 128
FAST = 8
SLOW = NSLOW // FAST
GROUP = 8
GROUPS = BINS // GROUP
BOTH = ("days", "chan")
NT = (((1,), (1,)), ((), ()))


def inverse_table():
    lag = np.arange(LAGS // 2)[:, None]
    freq = np.arange(BINS)[None, :]
    theta = (lag * freq % LAGS) * (2.0 * math.pi / LAGS)
    cosine, sine = np.cos(theta), np.sin(theta)
    sine[0] = 1 - 2 * (freq[0] % 2)
    table = np.concatenate([cosine, sine], 0) / math.sqrt(BINS)
    return table.astype(np.float32).astype(jnp.bfloat16)


def forward_table(scale):
    freq = np.arange(BINS)[:, None]
    lag = np.arange(LAGS // 2)[None, :]
    theta = (freq * lag % LAGS) * (2.0 * math.pi / LAGS)
    table = np.concatenate([np.cos(theta), -np.sin(theta)], 0) * scale
    high = table.astype(np.float32).astype(jnp.bfloat16)
    low = (table - high.astype(np.float64)).astype(np.float32).astype(jnp.bfloat16)
    return np.concatenate([high, low], 0)


def unit_circle(phase):
    quarter = PERIOD // 4
    turn = (phase + quarter // 2) >> 10
    angle = (phase - turn * quarter).astype(jnp.float32) * (2.0 * math.pi / PERIOD)
    square = angle * angle
    cosine = 1.0 + square * (-1 / 2 + square * (1 / 24 + square * (-1 / 720 + square * (1 / 40320))))
    sine = angle * (1.0 + square * (-1 / 6 + square * (1 / 120 + square * (-1 / 5040 + square * (1 / 362880)))))
    odd = (turn & 1) == 1
    real = jnp.where(odd, sine, cosine)
    imag = jnp.where(odd, cosine, sine)
    real = jnp.where(((turn + 1) & 2) == 2, -real, real)
    imag = jnp.where((turn & 2) == 2, -imag, imag)
    return real, imag


def times(left, right):
    return left[0] * right[0] - left[1] * right[1], left[0] * right[1] + left[1] * right[0]


def front_kernel(
    sources, offsets, spectra, inverse_far, forward_far,
    sent, steep, rotor, held, inverse, forward,
    places, spots, arrived,
):
    windows = spectra.shape[0]
    parts = 2 * BINS // LANES
    block = windows * parts
    peers = sent.shape[0] // block
    pairs = ((offsets, spots), (sources, places), (spectra, held), (inverse_far, inverse), (forward_far, forward))
    copies = [pltpu.make_async_copy(*pair, arrived.at[place]) for place, pair in enumerate(pairs)]
    for copy in copies:
        copy.start()

    copies[0].wait()
    chunk = 32
    for first in range(0, BINS, chunk):
        freq = first + lax.broadcasted_iota(jnp.int32, (chunk, LANES), 0)
        real, imag = unit_circle(freq * spots[...] & (PERIOD - 1))
        rotor[0, first : first + chunk, :] = real
        rotor[1, first : first + chunk, :] = imag
    across = jnp.transpose(jnp.broadcast_to(spots[...].astype(jnp.float32), (LANES, LANES))).astype(jnp.int32)
    lane = lax.broadcasted_iota(jnp.int32, (chunk, LANES), 1)
    for first in range(0, LANES, chunk):
        turn = across[first : first + chunk] * (lane // GROUP * FAST)
        value = unit_circle(turn * (lane & (GROUP - 1)) & (PERIOD - 1))
        step = unit_circle(turn * GROUP & (PERIOD - 1))
        for group in range(GROUPS):
            lanes = slice(group % 2 * LANES, (group % 2 + 1) * LANES)
            steep[group // 2, first : first + chunk, lanes] = value[0].astype(jnp.bfloat16)
            steep[group // 2, LANES + first : LANES + first + chunk, lanes] = value[1].astype(jnp.bfloat16)
            if group < GROUPS - 1:
                value = times(value, step)

    copies[1].wait()
    row = lax.broadcasted_iota(jnp.int32, (NSRC * block, LANES), 0)
    lane = lax.broadcasted_iota(jnp.int32, (NSRC * block, LANES), 1)
    column = jnp.where(row < block, places[:, 0:1], places[:, 1:2]) - lax.axis_index("chan") * LANES
    hit = jnp.where(lane == column, row & (block - 1), -1)
    total = jnp.zeros((NSRC * block, LANES), jnp.float32)
    copies[2].wait()
    for place in range(block):
        window, part = divmod(place, parts)
        chosen = jnp.where(hit == place, 1.0, 0.0).astype(jnp.bfloat16)
        piece = held[window, part * LANES : (part + 1) * LANES, :]
        total += lax.dot_general(chosen, piece, NT, preferred_element_type=jnp.float32)
    rounded = total.astype(jnp.bfloat16)
    half = peers // NSRC
    for peer in range(peers):
        source = peer // half
        sent[peer * block : (peer + 1) * block, :] = rounded[source * block : (source + 1) * block]
    copies[3].wait()
    copies[4].wait()


def main_kernel(
    scale,
    received, own, other, steep, rotor, inverse, forward,
    sent,
    cross, analytic, stack, turned, product,
):
    windows = own.shape[0]
    parts = 2 * BINS // LANES
    block = windows * parts
    half = received.shape[0] // block // NSRC
    day = lax.axis_index("days")
    picked = []
    for from_day in (day, 1 - day):
        total = None
        for peer in range(half):
            start = pl.multiple_of((from_day * half + peer) * block, block)
            term = received[pl.ds(start, block), :]
            total = term if peer == 0 else total + term
        picked.append(total.astype(jnp.float32))
    columns = jnp.transpose(jnp.concatenate(picked, 0))
    for window in range(2 * windows):
        taken = own if window < windows else other
        inner = window % windows
        for part in range(parts // 2):
            rows = slice(part * LANES, (part + 1) * LANES)
            below = slice(BINS + part * LANES, BINS + (part + 1) * LANES)
            place = window * parts + part
            real_s = jnp.broadcast_to(columns[:, place : place + 1], (LANES, LANES))
            place += parts // 2
            imag_s = jnp.broadcast_to(columns[:, place : place + 1], (LANES, LANES))
            real_x = taken[inner, rows, :].astype(jnp.float32)
            imag_x = taken[inner, below, :].astype(jnp.float32)
            cross[window, rows, :LANES] = (real_s * real_x + imag_s * imag_x).astype(jnp.bfloat16)
            cross[window, rows, LANES:] = (real_s * imag_x - imag_s * real_x).astype(jnp.bfloat16)

    for window in range(2 * windows):
        analytic[window] = jnp.dot(inverse[...], cross[window], preferred_element_type=jnp.float32)
    chunk = 16
    middle = LAGS // 2
    for first in range(0, middle, chunk):
        upper, lower = slice(first, first + chunk), slice(middle + first, middle + first + chunk)
        rising, falling = [None] * 3, [None] * 3
        for window in range(2 * windows):
            cos_re, cos_im = analytic[window, upper, :LANES], analytic[window, upper, LANES:]
            sin_re, sin_im = analytic[window, lower, :LANES], analytic[window, lower, LANES:]
            early = (cos_re - sin_im, cos_im + sin_re)
            late = (cos_re + sin_im, cos_im - sin_re)
            if first == 0:
                edge = lax.broadcasted_iota(jnp.int32, (chunk, LANES), 0) == 0
                early = (jnp.where(edge, cos_re, early[0]), jnp.where(edge, cos_im, early[1]))
                late = (jnp.where(edge, sin_re, late[0]), jnp.where(edge, sin_im, late[1]))
            for sums, (corr, hilb) in ((rising, early), (falling, late)):
                weight = lax.rsqrt(jnp.maximum(corr * corr + hilb * hilb, 0.25))
                for place, term in enumerate((corr, corr * weight, hilb * weight)):
                    sums[place] = term if window == 0 else sums[place] + term
        early, late = (sums[0] * (sums[1] * sums[1] + sums[2] * sums[2]) for sums in (rising, falling))
        if first == 0:
            turning = late[0:1, :] * scale
            late = jnp.where(edge, 0.0, late)
        for rows, weighted in ((upper, early + late), (lower, early - late)):
            large = weighted.astype(jnp.bfloat16)
            stack[rows, :LANES] = large
            stack[rows, LANES:] = (weighted - large.astype(jnp.float32)).astype(jnp.bfloat16)

    value = []
    for first in (0, BINS):
        rows = slice(first, first + BINS)
        wide = jnp.dot(forward[rows, :], stack[rows, :], preferred_element_type=jnp.float32)
        rest = slice(2 * BINS + first, 3 * BINS + first)
        value.append(
            wide[:, :LANES]
            + wide[:, LANES:]
            + jnp.dot(forward[rest, :], stack[rows, :LANES], preferred_element_type=jnp.float32)
        )
    odd = lax.broadcasted_iota(jnp.int32, (BINS, LANES), 0) & 1
    value[0] += jnp.where(odd == 1, -turning, turning)
    side = 2 * FAST * GROUP
    bin_lane = lax.broadcasted_iota(jnp.int32, (8, LANES), 1) & (GROUP - 1)
    spectrum = value
    kept = []
    for pair in range(GROUPS // 2):
        groups = slice(2 * pair, 2 * pair + 2)
        rows = slice(2 * pair * GROUP, 2 * (pair + 1) * GROUP)
        value = (spectrum[0][rows], spectrum[1][rows])
        base = (rotor[0, rows, :], rotor[1, rows, :])
        for fast in range(FAST):
            real = value[0].reshape(2, GROUP, LANES)
            imag = value[1].reshape(2, GROUP, LANES)
            turned[groups, fast, :, :LANES] = jnp.concatenate([real, imag], 1).astype(jnp.bfloat16)
            turned[groups, fast, :, LANES:] = jnp.concatenate([-imag, real], 1).astype(jnp.bfloat16)
            if fast < FAST - 1:
                value = times(value, base)
        both = turned[groups].reshape(2 * side, 2 * LANES)
        both = jnp.dot(both, steep[pair], preferred_element_type=jnp.float32)
        product[2 * pair] = both[:side, :LANES]
        product[2 * pair + 1] = both[side:, LANES:]
        for group in range(2 * pair, 2 * pair + 2):
            tiles = []
            for first in range(0, side, 8 * GROUP):
                tile = product[group, pl.ds(first, 8, stride=GROUP), :]
                for place in range(1, GROUP):
                    line = product[group, pl.ds(first + place, 8, stride=GROUP), :]
                    tile = jnp.where(bin_lane == place, line, tile)
                tiles.append(tile)
            kept.append(jnp.concatenate(tiles, 0))

    spot = lax.broadcasted_iota(jnp.int32, (2 * FAST, LANES), 1) // GROUP
    kept = [pltpu.roll(part, group % SLOW * GROUP, 1) if group % SLOW else part for group, part in enumerate(kept)]
    low_rows = lax.broadcasted_iota(jnp.int32, (8, LANES), 0) < 4
    for slow in range(SLOW):
        halves = []
        for first in (0, SLOW):
            joined = kept[first + -slow % SLOW]
            for place in range(1, SLOW):
                joined = jnp.where(spot == place, kept[first + (place - slow) % SLOW], joined)
            halves.append(pltpu.roll(joined, LANES - slow * GROUP, 1) if slow else joined)
        for pair in range(2):
            left = halves[0][8 * pair : 8 * pair + 8]
            right = halves[1][8 * pair : 8 * pair + 8]
            first = jnp.where(low_rows, left, pltpu.roll(right, 4, 0))
            second = jnp.where(low_rows, pltpu.roll(left, 4, 0), right)
            tile = jnp.concatenate([first, second], 0).astype(jnp.bfloat16)
            for day_side in range(2):
                start = (day_side * half + slow * (FAST // 2) + 2 * pair) * 8
                sent[start : start + 16, :] = tile


def sum_kernel(received, out):
    rows = received.shape[0] // NSRC
    for source in range(NSRC):
        terms = received[source * rows : (source + 1) * rows, :].astype(jnp.float32)
        total = jnp.sum(terms.reshape(rows // 8, 8, LANES), 0)
        for row in range(8):
            upper, slow, part = row // 4, row // 2 % 2, row % 2
            out[slow, source, part, upper * LANES : (upper + 1) * LANES] = total[row]


def in_hbm(array):
    return pltpu.with_memory_space_constraint(array, pltpu.HBM)


def shards(spectra, sources, offsets):
    windows = spectra.shape[0]
    width = spectra.shape[2]
    peers = lax.axis_size("days") * lax.axis_size("chan")
    all_windows = windows * lax.axis_size("days")
    channels = width * lax.axis_size("chan")
    scale = all_windows**1.5 / math.sqrt(channels) / all_windows**3
    scale /= math.sqrt(LAGS)
    forward = forward_table(scale)
    vmem = pl.BlockSpec(memory_space=pltpu.VMEM)
    far = pl.BlockSpec(memory_space=pltpu.HBM)
    block = windows * 2 * BINS // LANES

    other = lax.ppermute(spectra, "days", [(0, 1), (1, 0)])
    inverse = jnp.asarray(inverse_table())
    forward = jnp.asarray(forward)
    candidates, steep, rotor, own, inverse, forward = pl.pallas_call(
        front_kernel,
        out_shape=(
            jax.ShapeDtypeStruct((peers * block, LANES), jnp.bfloat16),
            jax.ShapeDtypeStruct((GROUPS // 2, 2 * LANES, 2 * LANES), jnp.bfloat16),
            jax.ShapeDtypeStruct((2, BINS, LANES), jnp.float32),
            jax.ShapeDtypeStruct(spectra.shape, jnp.bfloat16),
            jax.ShapeDtypeStruct(inverse.shape, jnp.bfloat16),
            jax.ShapeDtypeStruct(forward.shape, jnp.bfloat16),
        ),
        in_specs=[far] * 5,
        out_specs=(vmem,) * 6,
        scratch_shapes=[
            pltpu.VMEM((1, NSRC), jnp.int32),
            pltpu.VMEM((1, width), jnp.int32),
            pltpu.SemaphoreType.DMA((5,)),
        ],
        name="front",
        compiler_params=pltpu.CompilerParams(vmem_limit_bytes=8 << 20),
    )(
        in_hbm(sources.reshape(1, NSRC)),
        in_hbm(offsets.reshape(1, width)),
        in_hbm(spectra),
        in_hbm(inverse),
        in_hbm(forward),
    )
    received = lax.all_to_all(candidates.reshape(peers, block, LANES), BOTH, 0, 0, tiled=True)
    received = received.reshape(peers * block, LANES)
    terms = pl.pallas_call(
        functools.partial(main_kernel, scale),
        out_shape=jax.ShapeDtypeStruct((peers * 8, LANES), jnp.bfloat16),
        in_specs=[vmem] * 7,
        out_specs=vmem,
        scratch_shapes=[
            pltpu.VMEM((all_windows, BINS, 2 * LANES), jnp.bfloat16),
            pltpu.VMEM((all_windows, LAGS, 2 * LANES), jnp.float32),
            pltpu.VMEM((LAGS, 2 * LANES), jnp.bfloat16),
            pltpu.VMEM((GROUPS, FAST, 2 * GROUP, 2 * LANES), jnp.bfloat16),
            pltpu.VMEM((GROUPS, 2 * FAST * GROUP, LANES), jnp.float32),
        ],
        name="stack_and_slant",
        compiler_params=pltpu.CompilerParams(vmem_limit_bytes=24 << 20),
    )(received, own, other, steep, rotor, inverse, forward)
    partial = lax.all_to_all(terms.reshape(peers, 8, LANES), BOTH, 0, 0, tiled=True)
    return pl.pallas_call(
        sum_kernel,
        out_shape=jax.ShapeDtypeStruct((NSLOW // lax.axis_size("chan"), NSRC, 2, BINS), jnp.float32),
        in_specs=[vmem],
        out_specs=vmem,
        name="sum",
        compiler_params=pltpu.CompilerParams(vmem_limit_bytes=8 << 20),
    )(partial.reshape(peers * 8, LANES))


def solution(mesh):
    placed = (P("days", None, "chan"), P(), P("chan"))
    return jax.shard_map(
        shards, mesh=mesh, in_specs=placed, out_specs=P("chan", None, None, None), check_vma=False
    )
```

```python
import functools
import math

import jax
import jax.numpy as jnp
import numpy as np
from jax import lax
from jax.experimental import pallas as pl
from jax.experimental.pallas import tpu as pltpu
from jax.sharding import PartitionSpec as P

BINS = 256
LAGS = 512
NSLOW = 128
NSRC = 2
PERIOD = 4096
LANES = 128
FAST = 8
SLOW = NSLOW // FAST
GROUP = 8
GROUPS = BINS // GROUP
BOTH = ("days", "chan")
NT = (((1,), (1,)), ((), ()))


def inverse_table():
    lag = np.arange(LAGS // 2)[:, None]
    freq = np.arange(BINS)[None, :]
    theta = (lag * freq % LAGS) * (2.0 * math.pi / LAGS)
    cosine, sine = np.cos(theta), np.sin(theta)
    sine[0] = 1 - 2 * (freq[0] % 2)
    table = np.concatenate([cosine, sine], 0) / math.sqrt(BINS)
    return table.astype(np.float32).astype(jnp.bfloat16)


def forward_table(scale):
    freq = np.arange(BINS)[:, None]
    lag = np.arange(LAGS // 2)[None, :]
    theta = (freq * lag % LAGS) * (2.0 * math.pi / LAGS)
    table = np.concatenate([np.cos(theta), -np.sin(theta)], 0) * scale
    high = table.astype(np.float32).astype(jnp.bfloat16)
    low = (table - high.astype(np.float64)).astype(np.float32).astype(jnp.bfloat16)
    return np.concatenate([high, low], 0)


def unit_circle(phase):
    quarter = PERIOD // 4
    turn = (phase + quarter // 2) >> 10
    angle = (phase - turn * quarter).astype(jnp.float32) * (2.0 * math.pi / PERIOD)
    square = angle * angle
    cosine = 1.0 + square * (-1 / 2 + square * (1 / 24 + square * (-1 / 720 + square * (1 / 40320))))
    sine = angle * (1.0 + square * (-1 / 6 + square * (1 / 120 + square * (-1 / 5040 + square * (1 / 362880)))))
    odd = (turn & 1) == 1
    real = jnp.where(odd, sine, cosine)
    imag = jnp.where(odd, cosine, sine)
    real = jnp.where(((turn + 1) & 2) == 2, -real, real)
    imag = jnp.where((turn & 2) == 2, -imag, imag)
    return real, imag


def times(left, right):
    return left[0] * right[0] - left[1] * right[1], left[0] * right[1] + left[1] * right[0]


def front_kernel(
    sources, offsets, spectra, inverse_far, forward_far,
    sent, steep, rotor, held, inverse, forward,
    places, spots, arrived,
):
    windows = spectra.shape[0]
    parts = 2 * BINS // LANES
    block = windows * parts
    peers = sent.shape[0] // block
    pairs = ((offsets, spots), (sources, places), (spectra, held), (inverse_far, inverse), (forward_far, forward))
    copies = [pltpu.make_async_copy(*pair, arrived.at[place]) for place, pair in enumerate(pairs)]
    for copy in copies:
        copy.start()

    copies[0].wait()
    chunk = 32
    for first in range(0, BINS, chunk):
        freq = first + lax.broadcasted_iota(jnp.int32, (chunk, LANES), 0)
        real, imag = unit_circle(freq * spots[...] & (PERIOD - 1))
        rotor[0, first : first + chunk, :] = real
        rotor[1, first : first + chunk, :] = imag
    across = jnp.transpose(jnp.broadcast_to(spots[...].astype(jnp.float32), (LANES, LANES))).astype(jnp.int32)
    lane = lax.broadcasted_iota(jnp.int32, (chunk, LANES), 1)
    for first in range(0, LANES, chunk):
        turn = across[first : first + chunk] * (lane // GROUP * FAST)
        value = unit_circle(turn * (lane & (GROUP - 1)) & (PERIOD - 1))
        step = unit_circle(turn * GROUP & (PERIOD - 1))
        for group in range(GROUPS):
            lanes = slice(group % 2 * LANES, (group % 2 + 1) * LANES)
            steep[group // 2, first : first + chunk, lanes] = value[0].astype(jnp.bfloat16)
            steep[group // 2, LANES + first : LANES + first + chunk, lanes] = value[1].astype(jnp.bfloat16)
            if group < GROUPS - 1:
                value = times(value, step)

    copies[1].wait()
    row = lax.broadcasted_iota(jnp.int32, (NSRC * block, LANES), 0)
    lane = lax.broadcasted_iota(jnp.int32, (NSRC * block, LANES), 1)
    column = jnp.where(row < block, places[:, 0:1], places[:, 1:2]) - lax.axis_index("chan") * LANES
    hit = jnp.where(lane == column, row & (block - 1), -1)
    total = jnp.zeros((NSRC * block, LANES), jnp.float32)
    copies[2].wait()
    for place in range(block):
        window, part = divmod(place, parts)
        chosen = jnp.where(hit == place, 1.0, 0.0).astype(jnp.bfloat16)
        piece = held[window, part * LANES : (part + 1) * LANES, :]
        total += lax.dot_general(chosen, piece, NT, preferred_element_type=jnp.float32)
    rounded = total.astype(jnp.bfloat16)
    half = peers // NSRC
    for peer in range(peers):
        source = peer // half
        sent[peer * block : (peer + 1) * block, :] = rounded[source * block : (source + 1) * block]
    copies[3].wait()
    copies[4].wait()


def main_kernel(
    scale,
    received, own, other, steep, rotor, inverse, forward,
    sent,
    cross, analytic, stack, turned, product,
):
    windows = own.shape[0]
    parts = 2 * BINS // LANES
    block = windows * parts
    half = received.shape[0] // block // NSRC
    day = lax.axis_index("days")
    picked = []
    for from_day in (day, 1 - day):
        sums = [None] * 8
        for peer in range(half):
            start = pl.multiple_of((from_day * half + peer) * block, block)
            term = received[pl.ds(start, block), :]
            sums[peer % 8] = term if peer < 8 else sums[peer % 8] + term
        while len(sums) > 1:
            sums = [first + second for first, second in zip(sums[::2], sums[1::2])]
        picked.append(sums[0].astype(jnp.float32))
    columns = jnp.transpose(jnp.concatenate(picked, 0))
    for window in range(2 * windows):
        taken = own if window < windows else other
        inner = window % windows
        for part in range(parts // 2):
            rows = slice(part * LANES, (part + 1) * LANES)
            below = slice(BINS + part * LANES, BINS + (part + 1) * LANES)
            place = window * parts + part
            real_s = jnp.broadcast_to(columns[:, place : place + 1], (LANES, LANES))
            place += parts // 2
            imag_s = jnp.broadcast_to(columns[:, place : place + 1], (LANES, LANES))
            real_x = taken[inner, rows, :].astype(jnp.float32)
            imag_x = taken[inner, below, :].astype(jnp.float32)
            cross[window, rows, :LANES] = (real_s * real_x + imag_s * imag_x).astype(jnp.bfloat16)
            cross[window, rows, LANES:] = (real_s * imag_x - imag_s * real_x).astype(jnp.bfloat16)

    for window in range(2 * windows):
        analytic[window] = jnp.dot(inverse[...], cross[window], preferred_element_type=jnp.float32)
    chunk = 16
    middle = LAGS // 2
    for first in range(0, middle, chunk):
        upper, lower = slice(first, first + chunk), slice(middle + first, middle + first + chunk)
        rising, falling = [None] * 3, [None] * 3
        for window in range(2 * windows):
            cos_re, cos_im = analytic[window, upper, :LANES], analytic[window, upper, LANES:]
            sin_re, sin_im = analytic[window, lower, :LANES], analytic[window, lower, LANES:]
            early = (cos_re - sin_im, cos_im + sin_re)
            late = (cos_re + sin_im, cos_im - sin_re)
            if first == 0:
                edge = lax.broadcasted_iota(jnp.int32, (chunk, LANES), 0) == 0
                early = (jnp.where(edge, cos_re, early[0]), jnp.where(edge, cos_im, early[1]))
                late = (jnp.where(edge, sin_re, late[0]), jnp.where(edge, sin_im, late[1]))
            for sums, (corr, hilb) in ((rising, early), (falling, late)):
                weight = lax.rsqrt(jnp.maximum(corr * corr + hilb * hilb, 0.25))
                for place, term in enumerate((corr, corr * weight, hilb * weight)):
                    sums[place] = term if window == 0 else sums[place] + term
        early, late = (sums[0] * (sums[1] * sums[1] + sums[2] * sums[2]) for sums in (rising, falling))
        if first == 0:
            turning = late[0:1, :] * scale
            late = jnp.where(edge, 0.0, late)
        for rows, weighted in ((upper, early + late), (lower, early - late)):
            large = weighted.astype(jnp.bfloat16)
            stack[rows, :LANES] = large
            stack[rows, LANES:] = (weighted - large.astype(jnp.float32)).astype(jnp.bfloat16)

    value = []
    for first in (0, BINS):
        rows = slice(first, first + BINS)
        wide = jnp.dot(forward[rows, :], stack[rows, :], preferred_element_type=jnp.float32)
        rest = slice(2 * BINS + first, 3 * BINS + first)
        value.append(
            wide[:, :LANES]
            + wide[:, LANES:]
            + jnp.dot(forward[rest, :], stack[rows, :LANES], preferred_element_type=jnp.float32)
        )
    odd = lax.broadcasted_iota(jnp.int32, (BINS, LANES), 0) & 1
    value[0] += jnp.where(odd == 1, -turning, turning)
    side = 2 * FAST * GROUP
    bin_lane = lax.broadcasted_iota(jnp.int32, (8, LANES), 1) & (GROUP - 1)
    spectrum = value
    kept = []
    for pair in range(GROUPS // 2):
        groups = slice(2 * pair, 2 * pair + 2)
        rows = slice(2 * pair * GROUP, 2 * (pair + 1) * GROUP)
        value = (spectrum[0][rows], spectrum[1][rows])
        base = (rotor[0, rows, :], rotor[1, rows, :])
        for fast in range(FAST):
            real = value[0].reshape(2, GROUP, LANES)
            imag = value[1].reshape(2, GROUP, LANES)
            turned[groups, fast, :, :LANES] = jnp.concatenate([real, imag], 1).astype(jnp.bfloat16)
            turned[groups, fast, :, LANES:] = jnp.concatenate([-imag, real], 1).astype(jnp.bfloat16)
            if fast < FAST - 1:
                value = times(value, base)
        both = turned[groups].reshape(2 * side, 2 * LANES)
        both = jnp.dot(both, steep[pair], preferred_element_type=jnp.float32)
        product[2 * pair] = both[:side, :LANES]
        product[2 * pair + 1] = both[side:, LANES:]
        for group in range(2 * pair, 2 * pair + 2):
            tiles = []
            for first in range(0, side, 8 * GROUP):
                tile = product[group, pl.ds(first, 8, stride=GROUP), :]
                for place in range(1, GROUP):
                    line = product[group, pl.ds(first + place, 8, stride=GROUP), :]
                    tile = jnp.where(bin_lane == place, line, tile)
                tiles.append(tile)
            kept.append(jnp.concatenate(tiles, 0))

    spot = lax.broadcasted_iota(jnp.int32, (2 * FAST, LANES), 1) // GROUP
    kept = [pltpu.roll(part, group % SLOW * GROUP, 1) if group % SLOW else part for group, part in enumerate(kept)]
    low_rows = lax.broadcasted_iota(jnp.int32, (8, LANES), 0) < 4
    for slow in range(SLOW):
        halves = []
        for first in (0, SLOW):
            joined = kept[first + -slow % SLOW]
            for place in range(1, SLOW):
                joined = jnp.where(spot == place, kept[first + (place - slow) % SLOW], joined)
            halves.append(pltpu.roll(joined, LANES - slow * GROUP, 1) if slow else joined)
        for pair in range(2):
            left = halves[0][8 * pair : 8 * pair + 8]
            right = halves[1][8 * pair : 8 * pair + 8]
            first = jnp.where(low_rows, left, pltpu.roll(right, 4, 0))
            second = jnp.where(low_rows, pltpu.roll(left, 4, 0), right)
            tile = jnp.concatenate([first, second], 0).astype(jnp.bfloat16)
            for day_side in range(2):
                start = (day_side * half + slow * (FAST // 2) + 2 * pair) * 8
                sent[start : start + 16, :] = tile


def sum_kernel(received, out):
    rows = received.shape[0] // NSRC
    for source in range(NSRC):
        sums = [None] * 8
        for place in range(rows // 16):
            term = received[source * rows + place * 16 : source * rows + (place + 1) * 16, :].astype(jnp.float32)
            sums[place % 8] = term if place < 8 else sums[place % 8] + term
        while len(sums) > 1:
            sums = [first + second for first, second in zip(sums[::2], sums[1::2])]
        total = sums[0][:8] + sums[0][8:]
        for row in range(8):
            upper, slow, part = row // 4, row // 2 % 2, row % 2
            out[slow, source, part, upper * LANES : (upper + 1) * LANES] = total[row]


def in_hbm(array):
    return pltpu.with_memory_space_constraint(array, pltpu.HBM)


def shards(spectra, sources, offsets):
    windows = spectra.shape[0]
    width = spectra.shape[2]
    peers = lax.axis_size("days") * lax.axis_size("chan")
    all_windows = windows * lax.axis_size("days")
    channels = width * lax.axis_size("chan")
    scale = all_windows**1.5 / math.sqrt(channels) / all_windows**3
    scale /= math.sqrt(LAGS)
    forward = forward_table(scale)
    vmem = pl.BlockSpec(memory_space=pltpu.VMEM)
    far = pl.BlockSpec(memory_space=pltpu.HBM)
    block = windows * 2 * BINS // LANES

    other = lax.ppermute(spectra, "days", [(0, 1), (1, 0)])
    inverse = jnp.asarray(inverse_table())
    forward = jnp.asarray(forward)
    candidates, steep, rotor, own, inverse, forward = pl.pallas_call(
        front_kernel,
        out_shape=(
            jax.ShapeDtypeStruct((peers * block, LANES), jnp.bfloat16),
            jax.ShapeDtypeStruct((GROUPS // 2, 2 * LANES, 2 * LANES), jnp.bfloat16),
            jax.ShapeDtypeStruct((2, BINS, LANES), jnp.float32),
            jax.ShapeDtypeStruct(spectra.shape, jnp.bfloat16),
            jax.ShapeDtypeStruct(inverse.shape, jnp.bfloat16),
            jax.ShapeDtypeStruct(forward.shape, jnp.bfloat16),
        ),
        in_specs=[far] * 5,
        out_specs=(vmem,) * 6,
        scratch_shapes=[
            pltpu.VMEM((1, NSRC), jnp.int32),
            pltpu.VMEM((1, width), jnp.int32),
            pltpu.SemaphoreType.DMA((5,)),
        ],
        name="front",
        compiler_params=pltpu.CompilerParams(vmem_limit_bytes=8 << 20),
    )(
        in_hbm(sources.reshape(1, NSRC)),
        in_hbm(offsets.reshape(1, width)),
        in_hbm(spectra),
        in_hbm(inverse),
        in_hbm(forward),
    )
    received = lax.all_to_all(candidates.reshape(peers, block, LANES), BOTH, 0, 0, tiled=True)
    received = received.reshape(peers * block, LANES)
    terms = pl.pallas_call(
        functools.partial(main_kernel, scale),
        out_shape=jax.ShapeDtypeStruct((peers * 8, LANES), jnp.bfloat16),
        in_specs=[vmem] * 7,
        out_specs=vmem,
        scratch_shapes=[
            pltpu.VMEM((all_windows, BINS, 2 * LANES), jnp.bfloat16),
            pltpu.VMEM((all_windows, LAGS, 2 * LANES), jnp.float32),
            pltpu.VMEM((LAGS, 2 * LANES), jnp.bfloat16),
            pltpu.VMEM((GROUPS, FAST, 2 * GROUP, 2 * LANES), jnp.bfloat16),
            pltpu.VMEM((GROUPS, 2 * FAST * GROUP, LANES), jnp.float32),
        ],
        name="stack_and_slant",
        compiler_params=pltpu.CompilerParams(vmem_limit_bytes=24 << 20),
    )(received, own, other, steep, rotor, inverse, forward)
    partial = lax.all_to_all(terms.reshape(peers, 8, LANES), BOTH, 0, 0, tiled=True)
    return pl.pallas_call(
        sum_kernel,
        out_shape=jax.ShapeDtypeStruct((NSLOW // lax.axis_size("chan"), NSRC, 2, BINS), jnp.float32),
        in_specs=[vmem],
        out_specs=vmem,
        name="sum",
        compiler_params=pltpu.CompilerParams(vmem_limit_bytes=8 << 20),
    )(partial.reshape(peers * 8, LANES))


def solution(mesh):
    placed = (P("days", None, "chan"), P(), P("chan"))
    return jax.shard_map(
        shards, mesh=mesh, in_specs=placed, out_specs=P("chan", None, None, None), check_vma=False
    )
```

```python
import functools
import math

import jax
import jax.numpy as jnp
import numpy as np
from jax import lax
from jax.experimental import pallas as pl
from jax.experimental.pallas import tpu as pltpu
from jax.sharding import PartitionSpec as P

BINS = 256
LAGS = 512
NSLOW = 128
NSRC = 2
PERIOD = 4096
LANES = 128
FAST = 8
SLOW = NSLOW // FAST
GROUP = 8
GROUPS = BINS // GROUP
BOTH = ("days", "chan")
NT = (((1,), (1,)), ((), ()))


def inverse_table():
    lag = np.arange(LAGS // 2)[:, None]
    freq = np.arange(BINS)[None, :]
    theta = (lag * freq % LAGS) * (2.0 * math.pi / LAGS)
    cosine, sine = np.cos(theta), np.sin(theta)
    sine[0] = 1 - 2 * (freq[0] % 2)
    table = np.concatenate([cosine, sine], 0) / math.sqrt(BINS)
    return table.astype(np.float32).astype(jnp.bfloat16)


def forward_table(scale):
    freq = np.arange(BINS)[:, None]
    lag = np.arange(LAGS // 2)[None, :]
    theta = (freq * lag % LAGS) * (2.0 * math.pi / LAGS)
    table = np.concatenate([np.cos(theta), -np.sin(theta)], 0) * scale
    high = table.astype(np.float32).astype(jnp.bfloat16)
    low = (table - high.astype(np.float64)).astype(np.float32).astype(jnp.bfloat16)
    return np.concatenate([high, low], 0)


def unit_circle(phase):
    quarter = PERIOD // 4
    turn = (phase + quarter // 2) >> 10
    angle = (phase - turn * quarter).astype(jnp.float32) * (2.0 * math.pi / PERIOD)
    square = angle * angle
    cosine = 1.0 + square * (-1 / 2 + square * (1 / 24 + square * (-1 / 720 + square * (1 / 40320))))
    sine = angle * (1.0 + square * (-1 / 6 + square * (1 / 120 + square * (-1 / 5040 + square * (1 / 362880)))))
    odd = (turn & 1) == 1
    real = jnp.where(odd, sine, cosine)
    imag = jnp.where(odd, cosine, sine)
    real = jnp.where(((turn + 1) & 2) == 2, -real, real)
    imag = jnp.where((turn & 2) == 2, -imag, imag)
    return real, imag


def times(left, right):
    return left[0] * right[0] - left[1] * right[1], left[0] * right[1] + left[1] * right[0]


def front_kernel(
    sources, offsets, spectra, inverse_far, forward_far,
    sent, steep, rotor, held, inverse, forward,
    places, spots, arrived,
):
    windows = spectra.shape[0]
    parts = 2 * BINS // LANES
    block = windows * parts
    peers = sent.shape[0] // block
    pairs = ((offsets, spots), (sources, places), (spectra, held), (inverse_far, inverse), (forward_far, forward))
    copies = [pltpu.make_async_copy(*pair, arrived.at[place]) for place, pair in enumerate(pairs)]
    for copy in copies:
        copy.start()

    copies[0].wait()
    chunk = 32
    for first in range(0, BINS, chunk):
        freq = first + lax.broadcasted_iota(jnp.int32, (chunk, LANES), 0)
        real, imag = unit_circle(freq * spots[...] & (PERIOD - 1))
        rotor[0, first : first + chunk, :] = real
        rotor[1, first : first + chunk, :] = imag
    across = jnp.transpose(jnp.broadcast_to(spots[...].astype(jnp.float32), (LANES, LANES))).astype(jnp.int32)
    table_lane = lax.broadcasted_iota(jnp.int32, (chunk, LANES), 1)

    def place_powers(first):
        turn = across[first : first + chunk] * (table_lane // GROUP * FAST)
        value = unit_circle(turn * (table_lane & (GROUP - 1)) & (PERIOD - 1))
        step = unit_circle(turn * GROUP & (PERIOD - 1))
        for group in range(GROUPS):
            lanes = slice(group % 2 * LANES, (group % 2 + 1) * LANES)
            steep[group // 2, first : first + chunk, lanes] = value[0].astype(jnp.bfloat16)
            steep[group // 2, LANES + first : LANES + first + chunk, lanes] = value[1].astype(jnp.bfloat16)
            if group < GROUPS - 1:
                value = times(value, step)

    place_powers(0)
    place_powers(chunk)
    copies[1].wait()
    row = lax.broadcasted_iota(jnp.int32, (NSRC * block, LANES), 0)
    lane = lax.broadcasted_iota(jnp.int32, (NSRC * block, LANES), 1)
    column = jnp.where(row < block, places[:, 0:1], places[:, 1:2]) - lax.axis_index("chan") * LANES
    hit = jnp.where(lane == column, row & (block - 1), -1)
    copies[2].wait()
    sums = [None] * parts
    for place in range(block):
        window, part = divmod(place, parts)
        chosen = jnp.where(hit == place, 1.0, 0.0).astype(jnp.bfloat16)
        piece = held[window, part * LANES : (part + 1) * LANES, :]
        term = lax.dot_general(chosen, piece, NT, preferred_element_type=jnp.float32)
        sums[part] = term if window == 0 else sums[part] + term
        if place in (block // 2 - 1, block - 1):
            place_powers((2 + place * 2 // block) * chunk)
    total = sums[0]
    for term in sums[1:]:
        total += term
    rounded = total.astype(jnp.bfloat16)
    half = peers // NSRC
    for peer in range(peers):
        source = peer // half
        sent[peer * block : (peer + 1) * block, :] = rounded[source * block : (source + 1) * block]
    copies[3].wait()
    copies[4].wait()


def main_kernel(
    scale,
    received, own, other, steep, rotor, inverse, forward,
    sent,
    cross, analytic, stack, turned, product,
):
    windows = own.shape[0]
    parts = 2 * BINS // LANES
    block = windows * parts
    half = received.shape[0] // block // NSRC
    day = lax.axis_index("days")
    picked = []
    for from_day in (day, 1 - day):
        sums = [None] * 8
        for peer in range(half):
            start = pl.multiple_of((from_day * half + peer) * block, block)
            term = received[pl.ds(start, block), :]
            sums[peer % 8] = term if peer < 8 else sums[peer % 8] + term
        while len(sums) > 1:
            sums = [first + second for first, second in zip(sums[::2], sums[1::2])]
        picked.append(sums[0].astype(jnp.float32))
    columns = jnp.transpose(jnp.concatenate(picked, 0))
    for window in range(2 * windows):
        taken = own if window < windows else other
        inner = window % windows
        for part in range(parts // 2):
            rows = slice(part * LANES, (part + 1) * LANES)
            below = slice(BINS + part * LANES, BINS + (part + 1) * LANES)
            place = window * parts + part
            real_s = jnp.broadcast_to(columns[:, place : place + 1], (LANES, LANES))
            place += parts // 2
            imag_s = jnp.broadcast_to(columns[:, place : place + 1], (LANES, LANES))
            real_x = taken[inner, rows, :].astype(jnp.float32)
            imag_x = taken[inner, below, :].astype(jnp.float32)
            cross[window, rows, :LANES] = (real_s * real_x + imag_s * imag_x).astype(jnp.bfloat16)
            cross[window, rows, LANES:] = (real_s * imag_x - imag_s * real_x).astype(jnp.bfloat16)

    for window in range(2 * windows):
        analytic[window] = jnp.dot(inverse[...], cross[window], preferred_element_type=jnp.float32)
    chunk = 16
    middle = LAGS // 2
    for first in range(0, middle, chunk):
        upper, lower = slice(first, first + chunk), slice(middle + first, middle + first + chunk)
        rising, falling = [None] * 3, [None] * 3
        for window in range(2 * windows):
            cos_re, cos_im = analytic[window, upper, :LANES], analytic[window, upper, LANES:]
            sin_re, sin_im = analytic[window, lower, :LANES], analytic[window, lower, LANES:]
            early = (cos_re - sin_im, cos_im + sin_re)
            late = (cos_re + sin_im, cos_im - sin_re)
            if first == 0:
                edge = lax.broadcasted_iota(jnp.int32, (chunk, LANES), 0) == 0
                early = (jnp.where(edge, cos_re, early[0]), jnp.where(edge, cos_im, early[1]))
                late = (jnp.where(edge, sin_re, late[0]), jnp.where(edge, sin_im, late[1]))
            for sums, (corr, hilb) in ((rising, early), (falling, late)):
                weight = lax.rsqrt(jnp.maximum(corr * corr + hilb * hilb, 0.25))
                for place, term in enumerate((corr, corr * weight, hilb * weight)):
                    sums[place] = term if window == 0 else sums[place] + term
        early, late = (sums[0] * (sums[1] * sums[1] + sums[2] * sums[2]) for sums in (rising, falling))
        if first == 0:
            turning = late[0:1, :] * scale
            late = jnp.where(edge, 0.0, late)
        for rows, weighted in ((upper, early + late), (lower, early - late)):
            large = weighted.astype(jnp.bfloat16)
            stack[rows, :LANES] = large
            stack[rows, LANES:] = (weighted - large.astype(jnp.float32)).astype(jnp.bfloat16)

    value = []
    for first in (0, BINS):
        rows = slice(first, first + BINS)
        wide = jnp.dot(forward[rows, :], stack[rows, :], preferred_element_type=jnp.float32)
        rest = slice(2 * BINS + first, 3 * BINS + first)
        value.append(
            wide[:, :LANES]
            + wide[:, LANES:]
            + jnp.dot(forward[rest, :], stack[rows, :LANES], preferred_element_type=jnp.float32)
        )
    odd = lax.broadcasted_iota(jnp.int32, (BINS, LANES), 0) & 1
    value[0] += jnp.where(odd == 1, -turning, turning)
    side = 2 * FAST * GROUP
    bin_lane = lax.broadcasted_iota(jnp.int32, (8, LANES), 1) & (GROUP - 1)
    spectrum = value
    kept = []
    for pair in range(GROUPS // 2):
        groups = slice(2 * pair, 2 * pair + 2)
        rows = slice(2 * pair * GROUP, 2 * (pair + 1) * GROUP)
        value = (spectrum[0][rows], spectrum[1][rows])
        base = (rotor[0, rows, :], rotor[1, rows, :])
        for fast in range(FAST):
            real = value[0].reshape(2, GROUP, LANES)
            imag = value[1].reshape(2, GROUP, LANES)
            turned[groups, fast, :, :LANES] = jnp.concatenate([real, imag], 1).astype(jnp.bfloat16)
            turned[groups, fast, :, LANES:] = jnp.concatenate([-imag, real], 1).astype(jnp.bfloat16)
            if fast < FAST - 1:
                value = times(value, base)
        both = turned[groups].reshape(2 * side, 2 * LANES)
        both = jnp.dot(both, steep[pair], preferred_element_type=jnp.float32)
        product[2 * pair] = both[:side, :LANES]
        product[2 * pair + 1] = both[side:, LANES:]
        for group in range(2 * pair, 2 * pair + 2):
            tiles = []
            for first in range(0, side, 8 * GROUP):
                tile = product[group, pl.ds(first, 8, stride=GROUP), :]
                for place in range(1, GROUP):
                    line = product[group, pl.ds(first + place, 8, stride=GROUP), :]
                    tile = jnp.where(bin_lane == place, line, tile)
                tiles.append(tile)
            kept.append(jnp.concatenate(tiles, 0))

    spot = lax.broadcasted_iota(jnp.int32, (2 * FAST, LANES), 1) // GROUP
    kept = [pltpu.roll(part, group % SLOW * GROUP, 1) if group % SLOW else part for group, part in enumerate(kept)]
    low_rows = lax.broadcasted_iota(jnp.int32, (8, LANES), 0) < 4
    for slow in range(SLOW):
        halves = []
        for first in (0, SLOW):
            joined = kept[first + -slow % SLOW]
            for place in range(1, SLOW):
                joined = jnp.where(spot == place, kept[first + (place - slow) % SLOW], joined)
            halves.append(pltpu.roll(joined, LANES - slow * GROUP, 1) if slow else joined)
        for pair in range(2):
            left = halves[0][8 * pair : 8 * pair + 8]
            right = halves[1][8 * pair : 8 * pair + 8]
            first = jnp.where(low_rows, left, pltpu.roll(right, 4, 0))
            second = jnp.where(low_rows, pltpu.roll(left, 4, 0), right)
            tile = jnp.concatenate([first, second], 0).astype(jnp.bfloat16)
            for day_side in range(2):
                start = (day_side * half + slow * (FAST // 2) + 2 * pair) * 8
                sent[start : start + 16, :] = tile


def sum_kernel(received, out):
    rows = received.shape[0] // NSRC
    for source in range(NSRC):
        sums = [None] * 8
        for place in range(rows // 16):
            term = received[source * rows + place * 16 : source * rows + (place + 1) * 16, :].astype(jnp.float32)
            sums[place % 8] = term if place < 8 else sums[place % 8] + term
        while len(sums) > 1:
            sums = [first + second for first, second in zip(sums[::2], sums[1::2])]
        total = sums[0][:8] + sums[0][8:]
        for row in range(8):
            upper, slow, part = row // 4, row // 2 % 2, row % 2
            out[slow, source, part, upper * LANES : (upper + 1) * LANES] = total[row]


def in_hbm(array):
    return pltpu.with_memory_space_constraint(array, pltpu.HBM)


def shards(spectra, sources, offsets):
    windows = spectra.shape[0]
    width = spectra.shape[2]
    peers = lax.axis_size("days") * lax.axis_size("chan")
    all_windows = windows * lax.axis_size("days")
    channels = width * lax.axis_size("chan")
    scale = all_windows**1.5 / math.sqrt(channels) / all_windows**3
    scale /= math.sqrt(LAGS)
    forward = forward_table(scale)
    vmem = pl.BlockSpec(memory_space=pltpu.VMEM)
    far = pl.BlockSpec(memory_space=pltpu.HBM)
    block = windows * 2 * BINS // LANES

    other = lax.ppermute(spectra, "days", [(0, 1), (1, 0)])
    inverse = jnp.asarray(inverse_table())
    forward = jnp.asarray(forward)
    candidates, steep, rotor, own, inverse, forward = pl.pallas_call(
        front_kernel,
        out_shape=(
            jax.ShapeDtypeStruct((peers * block, LANES), jnp.bfloat16),
            jax.ShapeDtypeStruct((GROUPS // 2, 2 * LANES, 2 * LANES), jnp.bfloat16),
            jax.ShapeDtypeStruct((2, BINS, LANES), jnp.float32),
            jax.ShapeDtypeStruct(spectra.shape, jnp.bfloat16),
            jax.ShapeDtypeStruct(inverse.shape, jnp.bfloat16),
            jax.ShapeDtypeStruct(forward.shape, jnp.bfloat16),
        ),
        in_specs=[far] * 5,
        out_specs=(vmem,) * 6,
        scratch_shapes=[
            pltpu.VMEM((1, NSRC), jnp.int32),
            pltpu.VMEM((1, width), jnp.int32),
            pltpu.SemaphoreType.DMA((5,)),
        ],
        name="front",
        compiler_params=pltpu.CompilerParams(vmem_limit_bytes=8 << 20),
    )(
        in_hbm(sources.reshape(1, NSRC)),
        in_hbm(offsets.reshape(1, width)),
        in_hbm(spectra),
        in_hbm(inverse),
        in_hbm(forward),
    )
    received = lax.all_to_all(candidates.reshape(peers, block, LANES), BOTH, 0, 0, tiled=True)
    received = received.reshape(peers * block, LANES)
    terms = pl.pallas_call(
        functools.partial(main_kernel, scale),
        out_shape=jax.ShapeDtypeStruct((peers * 8, LANES), jnp.bfloat16),
        in_specs=[vmem] * 7,
        out_specs=vmem,
        scratch_shapes=[
            pltpu.VMEM((all_windows, BINS, 2 * LANES), jnp.bfloat16),
            pltpu.VMEM((all_windows, LAGS, 2 * LANES), jnp.float32),
            pltpu.VMEM((LAGS, 2 * LANES), jnp.bfloat16),
            pltpu.VMEM((GROUPS, FAST, 2 * GROUP, 2 * LANES), jnp.bfloat16),
            pltpu.VMEM((GROUPS, 2 * FAST * GROUP, LANES), jnp.float32),
        ],
        name="stack_and_slant",
        compiler_params=pltpu.CompilerParams(vmem_limit_bytes=24 << 20),
    )(received, own, other, steep, rotor, inverse, forward)
    partial = lax.all_to_all(terms.reshape(peers, 8, LANES), BOTH, 0, 0, tiled=True)
    return pl.pallas_call(
        sum_kernel,
        out_shape=jax.ShapeDtypeStruct((NSLOW // lax.axis_size("chan"), NSRC, 2, BINS), jnp.float32),
        in_specs=[vmem],
        out_specs=vmem,
        name="sum",
        compiler_params=pltpu.CompilerParams(vmem_limit_bytes=8 << 20),
    )(partial.reshape(peers * 8, LANES))


def solution(mesh):
    placed = (P("days", None, "chan"), P(), P("chan"))
    return jax.shard_map(
        shards, mesh=mesh, in_specs=placed, out_specs=P("chan", None, None, None), check_vma=False
    )
```

```python
import functools
import math

import jax
import jax.numpy as jnp
import numpy as np
from jax import lax
from jax.experimental import pallas as pl
from jax.experimental.pallas import tpu as pltpu
from jax.sharding import PartitionSpec as P

BINS = 256
LAGS = 512
NSLOW = 128
NSRC = 2
PERIOD = 4096
LANES = 128
FAST = 8
SLOW = NSLOW // FAST
GROUP = 8
GROUPS = BINS // GROUP
BOTH = ("days", "chan")
NT = (((1,), (1,)), ((), ()))


def inverse_table():
    lag = np.arange(LAGS // 2)[:, None]
    freq = np.arange(BINS)[None, :]
    theta = (lag * freq % LAGS) * (2.0 * math.pi / LAGS)
    cosine, sine = np.cos(theta), np.sin(theta)
    sine[0] = 1 - 2 * (freq[0] % 2)
    table = np.concatenate([cosine, sine], 0) / math.sqrt(BINS)
    return table.astype(np.float32).astype(jnp.bfloat16)


def forward_table(scale):
    freq = np.arange(BINS)[:, None]
    lag = np.arange(LAGS // 2)[None, :]
    theta = (freq * lag % LAGS) * (2.0 * math.pi / LAGS)
    table = np.concatenate([np.cos(theta), -np.sin(theta)], 0) * scale
    high = table.astype(np.float32).astype(jnp.bfloat16)
    low = (table - high.astype(np.float64)).astype(np.float32).astype(jnp.bfloat16)
    return np.concatenate([high, low], 0)


def unit_circle(phase):
    quarter = PERIOD // 4
    turn = (phase + quarter // 2) >> 10
    angle = (phase - turn * quarter).astype(jnp.float32) * (2.0 * math.pi / PERIOD)
    square = angle * angle
    cosine = 1.0 + square * (-1 / 2 + square * (1 / 24 + square * (-1 / 720 + square * (1 / 40320))))
    sine = angle * (1.0 + square * (-1 / 6 + square * (1 / 120 + square * (-1 / 5040 + square * (1 / 362880)))))
    odd = (turn & 1) == 1
    real = jnp.where(odd, sine, cosine)
    imag = jnp.where(odd, cosine, sine)
    real = jnp.where(((turn + 1) & 2) == 2, -real, real)
    imag = jnp.where((turn & 2) == 2, -imag, imag)
    return real, imag


def times(left, right):
    return left[0] * right[0] - left[1] * right[1], left[0] * right[1] + left[1] * right[0]


def front_kernel(
    sources, offsets, spectra, inverse_far, forward_far,
    sent, steep, rotor, held, inverse, forward,
    places, spots, arrived,
):
    windows = spectra.shape[0]
    parts = 2 * BINS // LANES
    block = windows * parts
    peers = sent.shape[0] // block
    pairs = ((offsets, spots), (sources, places), (spectra, held), (inverse_far, inverse), (forward_far, forward))
    copies = [pltpu.make_async_copy(*pair, arrived.at[place]) for place, pair in enumerate(pairs)]
    for copy in copies:
        copy.start()

    copies[0].wait()
    chunk = 32
    for first in range(0, BINS, chunk):
        freq = first + lax.broadcasted_iota(jnp.int32, (chunk, LANES), 0)
        real, imag = unit_circle(freq * spots[...] & (PERIOD - 1))
        rotor[0, first : first + chunk, :] = real
        rotor[1, first : first + chunk, :] = imag
    across = jnp.transpose(jnp.broadcast_to(spots[...].astype(jnp.float32), (LANES, LANES))).astype(jnp.int32)
    table_lane = lax.broadcasted_iota(jnp.int32, (chunk, LANES), 1)

    def place_powers(first):
        turn = across[first : first + chunk] * (table_lane // GROUP * FAST)
        value = unit_circle(turn * (table_lane & (GROUP - 1)) & (PERIOD - 1))
        step = unit_circle(turn * GROUP & (PERIOD - 1))
        for group in range(GROUPS):
            lanes = slice(group % 2 * LANES, (group % 2 + 1) * LANES)
            steep[group // 2, first : first + chunk, lanes] = value[0].astype(jnp.bfloat16)
            steep[group // 2, LANES + first : LANES + first + chunk, lanes] = value[1].astype(jnp.bfloat16)
            if group < GROUPS - 1:
                value = times(value, step)

    place_powers(0)
    place_powers(chunk)
    copies[1].wait()
    row = lax.broadcasted_iota(jnp.int32, (NSRC * block, LANES), 0)
    lane = lax.broadcasted_iota(jnp.int32, (NSRC * block, LANES), 1)
    column = jnp.where(row < block, places[:, 0:1], places[:, 1:2]) - lax.axis_index("chan") * LANES
    hit = jnp.where(lane == column, row & (block - 1), -1)
    copies[2].wait()
    sums = [None] * parts
    for place in range(block):
        window, part = divmod(place, parts)
        chosen = jnp.where(hit == place, 1.0, 0.0).astype(jnp.bfloat16)
        piece = held[window, part * LANES : (part + 1) * LANES, :]
        term = lax.dot_general(chosen, piece, NT, preferred_element_type=jnp.float32)
        sums[part] = term if window == 0 else sums[part] + term
        if place in (block // 2 - 1, block - 1):
            place_powers((2 + place * 2 // block) * chunk)
    total = sums[0]
    for term in sums[1:]:
        total += term
    rounded = total.astype(jnp.bfloat16)
    half = peers // NSRC
    for peer in range(peers):
        source = peer // half
        sent[peer * block : (peer + 1) * block, :] = rounded[source * block : (source + 1) * block]
    copies[3].wait()
    copies[4].wait()


def main_kernel(
    scale,
    received, own, other, steep, rotor, inverse, forward,
    sent,
    cross, analytic, stack, product,
):
    windows = own.shape[0]
    parts = 2 * BINS // LANES
    block = windows * parts
    half = received.shape[0] // block // NSRC
    day = lax.axis_index("days")
    picked = []
    for from_day in (day, 1 - day):
        sums = [None] * 8
        for peer in range(half):
            start = pl.multiple_of((from_day * half + peer) * block, block)
            term = received[pl.ds(start, block), :]
            sums[peer % 8] = term if peer < 8 else sums[peer % 8] + term
        while len(sums) > 1:
            sums = [first + second for first, second in zip(sums[::2], sums[1::2])]
        picked.append(sums[0].astype(jnp.float32))
    columns = jnp.transpose(jnp.concatenate(picked, 0))
    for window in range(2 * windows):
        taken = own if window < windows else other
        inner = window % windows
        for part in range(parts // 2):
            rows = slice(part * LANES, (part + 1) * LANES)
            below = slice(BINS + part * LANES, BINS + (part + 1) * LANES)
            place = window * parts + part
            real_s = jnp.broadcast_to(columns[:, place : place + 1], (LANES, LANES))
            place += parts // 2
            imag_s = jnp.broadcast_to(columns[:, place : place + 1], (LANES, LANES))
            real_x = taken[inner, rows, :].astype(jnp.float32)
            imag_x = taken[inner, below, :].astype(jnp.float32)
            cross[window, rows, :LANES] = (real_s * real_x + imag_s * imag_x).astype(jnp.bfloat16)
            cross[window, rows, LANES:] = (real_s * imag_x - imag_s * real_x).astype(jnp.bfloat16)

    for window in range(2 * windows):
        analytic[window] = jnp.dot(inverse[...], cross[window], preferred_element_type=jnp.float32)
    chunk = 16
    middle = LAGS // 2
    for first in range(0, middle, chunk):
        upper, lower = slice(first, first + chunk), slice(middle + first, middle + first + chunk)
        rising, falling = [None] * 3, [None] * 3
        for window in range(2 * windows):
            cos_re, cos_im = analytic[window, upper, :LANES], analytic[window, upper, LANES:]
            sin_re, sin_im = analytic[window, lower, :LANES], analytic[window, lower, LANES:]
            early = (cos_re - sin_im, cos_im + sin_re)
            late = (cos_re + sin_im, cos_im - sin_re)
            if first == 0:
                edge = lax.broadcasted_iota(jnp.int32, (chunk, LANES), 0) == 0
                early = (jnp.where(edge, cos_re, early[0]), jnp.where(edge, cos_im, early[1]))
                late = (jnp.where(edge, sin_re, late[0]), jnp.where(edge, sin_im, late[1]))
            for sums, (corr, hilb) in ((rising, early), (falling, late)):
                weight = lax.rsqrt(jnp.maximum(corr * corr + hilb * hilb, 0.25))
                for place, term in enumerate((corr, corr * weight, hilb * weight)):
                    sums[place] = term if window == 0 else sums[place] + term
        early, late = (sums[0] * (sums[1] * sums[1] + sums[2] * sums[2]) for sums in (rising, falling))
        if first == 0:
            turning = late[0:1, :] * scale
            late = jnp.where(edge, 0.0, late)
        for rows, weighted in ((upper, early + late), (lower, early - late)):
            large = weighted.astype(jnp.bfloat16)
            stack[rows, :LANES] = large
            stack[rows, LANES:] = (weighted - large.astype(jnp.float32)).astype(jnp.bfloat16)

    value = []
    for first in (0, BINS):
        rows = slice(first, first + BINS)
        wide = jnp.dot(forward[rows, :], stack[rows, :], preferred_element_type=jnp.float32)
        rest = slice(2 * BINS + first, 3 * BINS + first)
        value.append(
            wide[:, :LANES]
            + wide[:, LANES:]
            + jnp.dot(forward[rest, :], stack[rows, :LANES], preferred_element_type=jnp.float32)
        )
    odd = lax.broadcasted_iota(jnp.int32, (BINS, LANES), 0) & 1
    value[0] += jnp.where(odd == 1, -turning, turning)
    side = 2 * FAST * GROUP
    bin_lane = lax.broadcasted_iota(jnp.int32, (8, LANES), 1) & (GROUP - 1)
    spectrum = value
    kept = []
    for pair in range(GROUPS // 2):
        groups = slice(2 * pair, 2 * pair + 2)
        rows = slice(2 * pair * GROUP, 2 * (pair + 1) * GROUP)
        value = (spectrum[0][rows], spectrum[1][rows])
        base = (rotor[0, rows, :], rotor[1, rows, :])
        lines = ([], [])
        for fast in range(FAST):
            for group in range(2):
                bins = slice(group * GROUP, (group + 1) * GROUP)
                real, imag = value[0][bins], value[1][bins]
                left = jnp.concatenate([real, imag], 0).astype(jnp.bfloat16)
                right = jnp.concatenate([-imag, real], 0).astype(jnp.bfloat16)
                lines[group].append(jnp.concatenate([left, right], 1))
            if fast < FAST - 1:
                value = times(value, base)
        both = jnp.concatenate(lines[0] + lines[1], 0)
        both = jnp.dot(both, steep[pair], preferred_element_type=jnp.float32)
        product[2 * pair] = both[:side, :LANES]
        product[2 * pair + 1] = both[side:, LANES:]
        for group in range(2 * pair, 2 * pair + 2):
            tiles = []
            for first in range(0, side, 8 * GROUP):
                tile = product[group, pl.ds(first, 8, stride=GROUP), :]
                for place in range(1, GROUP):
                    line = product[group, pl.ds(first + place, 8, stride=GROUP), :]
                    tile = jnp.where(bin_lane == place, line, tile)
                tiles.append(tile)
            kept.append(jnp.concatenate(tiles, 0))

    spot = lax.broadcasted_iota(jnp.int32, (2 * FAST, LANES), 1) // GROUP
    kept = [pltpu.roll(part, group % SLOW * GROUP, 1) if group % SLOW else part for group, part in enumerate(kept)]
    low_rows = lax.broadcasted_iota(jnp.int32, (8, LANES), 0) < 4
    for slow in range(SLOW):
        halves = []
        for first in (0, SLOW):
            joined = kept[first + -slow % SLOW]
            for place in range(1, SLOW):
                joined = jnp.where(spot == place, kept[first + (place - slow) % SLOW], joined)
            halves.append(pltpu.roll(joined, LANES - slow * GROUP, 1) if slow else joined)
        for pair in range(2):
            left = halves[0][8 * pair : 8 * pair + 8]
            right = halves[1][8 * pair : 8 * pair + 8]
            first = jnp.where(low_rows, left, pltpu.roll(right, 4, 0))
            second = jnp.where(low_rows, pltpu.roll(left, 4, 0), right)
            tile = jnp.concatenate([first, second], 0).astype(jnp.bfloat16)
            for day_side in range(2):
                start = (day_side * half + slow * (FAST // 2) + 2 * pair) * 8
                sent[start : start + 16, :] = tile


def sum_kernel(received, out):
    rows = received.shape[0] // NSRC
    for source in range(NSRC):
        sums = [None] * 8
        for place in range(rows // 16):
            term = received[source * rows + place * 16 : source * rows + (place + 1) * 16, :].astype(jnp.float32)
            sums[place % 8] = term if place < 8 else sums[place % 8] + term
        while len(sums) > 1:
            sums = [first + second for first, second in zip(sums[::2], sums[1::2])]
        total = sums[0][:8] + sums[0][8:]
        for row in range(8):
            upper, slow, part = row // 4, row // 2 % 2, row % 2
            out[slow, source, part, upper * LANES : (upper + 1) * LANES] = total[row]


def in_hbm(array):
    return pltpu.with_memory_space_constraint(array, pltpu.HBM)


def shards(spectra, sources, offsets):
    windows = spectra.shape[0]
    width = spectra.shape[2]
    peers = lax.axis_size("days") * lax.axis_size("chan")
    all_windows = windows * lax.axis_size("days")
    channels = width * lax.axis_size("chan")
    scale = all_windows**1.5 / math.sqrt(channels) / all_windows**3
    scale /= math.sqrt(LAGS)
    forward = forward_table(scale)
    vmem = pl.BlockSpec(memory_space=pltpu.VMEM)
    far = pl.BlockSpec(memory_space=pltpu.HBM)
    block = windows * 2 * BINS // LANES

    other = lax.ppermute(spectra, "days", [(0, 1), (1, 0)])
    inverse = jnp.asarray(inverse_table())
    forward = jnp.asarray(forward)
    candidates, steep, rotor, own, inverse, forward = pl.pallas_call(
        front_kernel,
        out_shape=(
            jax.ShapeDtypeStruct((peers * block, LANES), jnp.bfloat16),
            jax.ShapeDtypeStruct((GROUPS // 2, 2 * LANES, 2 * LANES), jnp.bfloat16),
            jax.ShapeDtypeStruct((2, BINS, LANES), jnp.float32),
            jax.ShapeDtypeStruct(spectra.shape, jnp.bfloat16),
            jax.ShapeDtypeStruct(inverse.shape, jnp.bfloat16),
            jax.ShapeDtypeStruct(forward.shape, jnp.bfloat16),
        ),
        in_specs=[far] * 5,
        out_specs=(vmem,) * 6,
        scratch_shapes=[
            pltpu.VMEM((1, NSRC), jnp.int32),
            pltpu.VMEM((1, width), jnp.int32),
            pltpu.SemaphoreType.DMA((5,)),
        ],
        name="front",
        compiler_params=pltpu.CompilerParams(vmem_limit_bytes=8 << 20),
    )(
        in_hbm(sources.reshape(1, NSRC)),
        in_hbm(offsets.reshape(1, width)),
        in_hbm(spectra),
        in_hbm(inverse),
        in_hbm(forward),
    )
    received = lax.all_to_all(candidates.reshape(peers, block, LANES), BOTH, 0, 0, tiled=True)
    received = received.reshape(peers * block, LANES)
    terms = pl.pallas_call(
        functools.partial(main_kernel, scale),
        out_shape=jax.ShapeDtypeStruct((peers * 8, LANES), jnp.bfloat16),
        in_specs=[vmem] * 7,
        out_specs=vmem,
        scratch_shapes=[
            pltpu.VMEM((all_windows, BINS, 2 * LANES), jnp.bfloat16),
            pltpu.VMEM((all_windows, LAGS, 2 * LANES), jnp.float32),
            pltpu.VMEM((LAGS, 2 * LANES), jnp.bfloat16),
            pltpu.VMEM((GROUPS, 2 * FAST * GROUP, LANES), jnp.float32),
        ],
        name="stack_and_slant",
        compiler_params=pltpu.CompilerParams(vmem_limit_bytes=24 << 20),
    )(received, own, other, steep, rotor, inverse, forward)
    partial = lax.all_to_all(terms.reshape(peers, 8, LANES), BOTH, 0, 0, tiled=True)
    return pl.pallas_call(
        sum_kernel,
        out_shape=jax.ShapeDtypeStruct((NSLOW // lax.axis_size("chan"), NSRC, 2, BINS), jnp.float32),
        in_specs=[vmem],
        out_specs=vmem,
        name="sum",
        compiler_params=pltpu.CompilerParams(vmem_limit_bytes=8 << 20),
    )(partial.reshape(peers * 8, LANES))


def solution(mesh):
    placed = (P("days", None, "chan"), P(), P("chan"))
    return jax.shard_map(
        shards, mesh=mesh, in_specs=placed, out_specs=P("chan", None, None, None), check_vma=False
    )
```

```python
import functools
import math

import jax
import jax.numpy as jnp
import numpy as np
from jax import lax
from jax.experimental import pallas as pl
from jax.experimental.pallas import tpu as pltpu
from jax.sharding import PartitionSpec as P

BINS = 256
LAGS = 512
NSLOW = 128
NSRC = 2
PERIOD = 4096
LANES = 128
FAST = 8
SLOW = NSLOW // FAST
GROUP = 8
GROUPS = BINS // GROUP
BOTH = ("days", "chan")
NT = (((1,), (1,)), ((), ()))


def inverse_table():
    lag = np.arange(LAGS // 2)[:, None]
    freq = np.arange(BINS)[None, :]
    theta = (lag * freq % LAGS) * (2.0 * math.pi / LAGS)
    cosine, sine = np.cos(theta), np.sin(theta)
    sine[0] = 1 - 2 * (freq[0] % 2)
    table = np.concatenate([cosine, sine], 0) / math.sqrt(BINS)
    return table.astype(np.float32).astype(jnp.bfloat16)


def forward_table(scale):
    freq = np.arange(BINS)[:, None]
    lag = np.arange(LAGS // 2)[None, :]
    theta = (freq * lag % LAGS) * (2.0 * math.pi / LAGS)
    table = np.concatenate([np.cos(theta), -np.sin(theta)], 0) * scale
    high = table.astype(np.float32).astype(jnp.bfloat16)
    low = (table - high.astype(np.float64)).astype(np.float32).astype(jnp.bfloat16)
    return np.concatenate([high, low], 0)


def unit_circle(phase):
    quarter = PERIOD // 4
    turn = (phase + quarter // 2) >> 10
    angle = (phase - turn * quarter).astype(jnp.float32) * (2.0 * math.pi / PERIOD)
    square = angle * angle
    cosine = 1.0 + square * (-1 / 2 + square * (1 / 24 + square * (-1 / 720 + square * (1 / 40320))))
    sine = angle * (1.0 + square * (-1 / 6 + square * (1 / 120 + square * (-1 / 5040 + square * (1 / 362880)))))
    odd = (turn & 1) == 1
    real = jnp.where(odd, sine, cosine)
    imag = jnp.where(odd, cosine, sine)
    real = jnp.where(((turn + 1) & 2) == 2, -real, real)
    imag = jnp.where((turn & 2) == 2, -imag, imag)
    return real, imag


def times(left, right):
    return left[0] * right[0] - left[1] * right[1], left[0] * right[1] + left[1] * right[0]


def front_kernel(
    sources, offsets, spectra, inverse_far, forward_far,
    sent, steep, rotor, held, inverse, forward,
    places, spots, arrived,
):
    windows = spectra.shape[0]
    parts = 2 * BINS // LANES
    block = windows * parts
    peers = sent.shape[0] // block
    pairs = ((offsets, spots), (sources, places), (spectra, held), (inverse_far, inverse), (forward_far, forward))
    copies = [pltpu.make_async_copy(*pair, arrived.at[place]) for place, pair in enumerate(pairs)]
    for copy in copies:
        copy.start()

    copies[0].wait()
    chunk = 32
    for first in range(0, BINS, chunk):
        freq = first + lax.broadcasted_iota(jnp.int32, (chunk, LANES), 0)
        real, imag = unit_circle(freq * spots[...] & (PERIOD - 1))
        rotor[0, first : first + chunk, :] = real
        rotor[1, first : first + chunk, :] = imag
    across = jnp.transpose(jnp.broadcast_to(spots[...].astype(jnp.float32), (LANES, LANES))).astype(jnp.int32)
    table_lane = lax.broadcasted_iota(jnp.int32, (chunk, LANES), 1)

    def place_powers(first):
        turn = across[first : first + chunk] * (table_lane // GROUP * FAST)
        value = unit_circle(turn * (table_lane & (GROUP - 1)) & (PERIOD - 1))
        step = unit_circle(turn * GROUP & (PERIOD - 1))
        for group in range(GROUPS):
            lanes = slice(group % 2 * LANES, (group % 2 + 1) * LANES)
            steep[group // 2, first : first + chunk, lanes] = value[0].astype(jnp.bfloat16)
            steep[group // 2, LANES + first : LANES + first + chunk, lanes] = value[1].astype(jnp.bfloat16)
            if group < GROUPS - 1:
                value = times(value, step)

    place_powers(0)
    place_powers(chunk)
    copies[1].wait()
    row = lax.broadcasted_iota(jnp.int32, (NSRC * block, LANES), 0)
    lane = lax.broadcasted_iota(jnp.int32, (NSRC * block, LANES), 1)
    column = jnp.where(row < block, places[:, 0:1], places[:, 1:2]) - lax.axis_index("chan") * LANES
    hit = jnp.where(lane == column, row & (block - 1), -1)
    copies[2].wait()
    sums = [None] * parts
    for place in range(block):
        window, part = divmod(place, parts)
        chosen = jnp.where(hit == place, 1.0, 0.0).astype(jnp.bfloat16)
        piece = held[window, part * LANES : (part + 1) * LANES, :]
        term = lax.dot_general(chosen, piece, NT, preferred_element_type=jnp.float32)
        sums[part] = term if window == 0 else sums[part] + term
        if place in (block // 2 - 1, block - 1):
            place_powers((2 + place * 2 // block) * chunk)
    total = sums[0]
    for term in sums[1:]:
        total += term
    rounded = total.astype(jnp.bfloat16)
    half = peers // NSRC
    for peer in range(peers):
        source = peer // half
        sent[peer * block : (peer + 1) * block, :] = rounded[source * block : (source + 1) * block]
    copies[3].wait()
    copies[4].wait()


def main_kernel(
    scale,
    received, own, other, steep, rotor, inverse, forward,
    sent,
    analytic, stack, product,
):
    windows = own.shape[0]
    parts = 2 * BINS // LANES
    block = windows * parts
    half = received.shape[0] // block // NSRC
    day = lax.axis_index("days")
    picked = []
    for from_day in (day, 1 - day):
        sums = [None] * 8
        for peer in range(half):
            start = pl.multiple_of((from_day * half + peer) * block, block)
            term = received[pl.ds(start, block), :]
            sums[peer % 8] = term if peer < 8 else sums[peer % 8] + term
        while len(sums) > 1:
            sums = [first + second for first, second in zip(sums[::2], sums[1::2])]
        picked.append(sums[0].astype(jnp.float32))
    columns = jnp.transpose(jnp.concatenate(picked, 0))
    for window in range(2 * windows):
        taken = own if window < windows else other
        inner = window % windows
        crossed = []
        for part in range(parts // 2):
            rows = slice(part * LANES, (part + 1) * LANES)
            below = slice(BINS + part * LANES, BINS + (part + 1) * LANES)
            place = window * parts + part
            real_s = jnp.broadcast_to(columns[:, place : place + 1], (LANES, LANES))
            place += parts // 2
            imag_s = jnp.broadcast_to(columns[:, place : place + 1], (LANES, LANES))
            real_x = taken[inner, rows, :].astype(jnp.float32)
            imag_x = taken[inner, below, :].astype(jnp.float32)
            real = (real_s * real_x + imag_s * imag_x).astype(jnp.bfloat16)
            imag = (real_s * imag_x - imag_s * real_x).astype(jnp.bfloat16)
            crossed.append(jnp.concatenate([real, imag], 1))
        crossed = jnp.concatenate(crossed, 0)
        analytic[window] = jnp.dot(inverse[...], crossed, preferred_element_type=jnp.float32)
    chunk = 16
    middle = LAGS // 2
    for first in range(0, middle, chunk):
        upper, lower = slice(first, first + chunk), slice(middle + first, middle + first + chunk)
        rising, falling = [None] * 3, [None] * 3
        for window in range(2 * windows):
            cos_re, cos_im = analytic[window, upper, :LANES], analytic[window, upper, LANES:]
            sin_re, sin_im = analytic[window, lower, :LANES], analytic[window, lower, LANES:]
            early = (cos_re - sin_im, cos_im + sin_re)
            late = (cos_re + sin_im, cos_im - sin_re)
            if first == 0:
                edge = lax.broadcasted_iota(jnp.int32, (chunk, LANES), 0) == 0
                early = (jnp.where(edge, cos_re, early[0]), jnp.where(edge, cos_im, early[1]))
                late = (jnp.where(edge, sin_re, late[0]), jnp.where(edge, sin_im, late[1]))
            for sums, (corr, hilb) in ((rising, early), (falling, late)):
                weight = lax.rsqrt(jnp.maximum(corr * corr + hilb * hilb, 0.25))
                for place, term in enumerate((corr, corr * weight, hilb * weight)):
                    sums[place] = term if window == 0 else sums[place] + term
        early, late = (sums[0] * (sums[1] * sums[1] + sums[2] * sums[2]) for sums in (rising, falling))
        if first == 0:
            turning = late[0:1, :] * scale
            late = jnp.where(edge, 0.0, late)
        for rows, weighted in ((upper, early + late), (lower, early - late)):
            large = weighted.astype(jnp.bfloat16)
            stack[rows, :LANES] = large
            stack[rows, LANES:] = (weighted - large.astype(jnp.float32)).astype(jnp.bfloat16)

    value = []
    for first in (0, BINS):
        rows = slice(first, first + BINS)
        wide = jnp.dot(forward[rows, :], stack[rows, :], preferred_element_type=jnp.float32)
        rest = slice(2 * BINS + first, 3 * BINS + first)
        value.append(
            wide[:, :LANES]
            + wide[:, LANES:]
            + jnp.dot(forward[rest, :], stack[rows, :LANES], preferred_element_type=jnp.float32)
        )
    odd = lax.broadcasted_iota(jnp.int32, (BINS, LANES), 0) & 1
    value[0] += jnp.where(odd == 1, -turning, turning)
    side = 2 * FAST * GROUP
    bin_lane = lax.broadcasted_iota(jnp.int32, (8, LANES), 1) & (GROUP - 1)
    spectrum = value
    kept = []
    for pair in range(GROUPS // 2):
        groups = slice(2 * pair, 2 * pair + 2)
        rows = slice(2 * pair * GROUP, 2 * (pair + 1) * GROUP)
        value = (spectrum[0][rows], spectrum[1][rows])
        base = (rotor[0, rows, :], rotor[1, rows, :])
        lines = ([], [])
        for fast in range(FAST):
            for group in range(2):
                bins = slice(group * GROUP, (group + 1) * GROUP)
                real, imag = value[0][bins], value[1][bins]
                left = jnp.concatenate([real, imag], 0).astype(jnp.bfloat16)
                right = jnp.concatenate([-imag, real], 0).astype(jnp.bfloat16)
                lines[group].append(jnp.concatenate([left, right], 1))
            if fast < FAST - 1:
                value = times(value, base)
        both = jnp.concatenate(lines[0] + lines[1], 0)
        both = jnp.dot(both, steep[pair], preferred_element_type=jnp.float32)
        product[2 * pair] = both[:side, :LANES]
        product[2 * pair + 1] = both[side:, LANES:]
        for group in range(2 * pair, 2 * pair + 2):
            tiles = []
            for first in range(0, side, 8 * GROUP):
                tile = product[group, pl.ds(first, 8, stride=GROUP), :]
                for place in range(1, GROUP):
                    line = product[group, pl.ds(first + place, 8, stride=GROUP), :]
                    tile = jnp.where(bin_lane == place, line, tile)
                tiles.append(tile)
            kept.append(jnp.concatenate(tiles, 0))

    spot = lax.broadcasted_iota(jnp.int32, (2 * FAST, LANES), 1) // GROUP
    kept = [pltpu.roll(part, group % SLOW * GROUP, 1) if group % SLOW else part for group, part in enumerate(kept)]
    low_rows = lax.broadcasted_iota(jnp.int32, (8, LANES), 0) < 4
    for slow in range(SLOW):
        halves = []
        for first in (0, SLOW):
            joined = kept[first + -slow % SLOW]
            for place in range(1, SLOW):
                joined = jnp.where(spot == place, kept[first + (place - slow) % SLOW], joined)
            halves.append(pltpu.roll(joined, LANES - slow * GROUP, 1) if slow else joined)
        for pair in range(2):
            left = halves[0][8 * pair : 8 * pair + 8]
            right = halves[1][8 * pair : 8 * pair + 8]
            first = jnp.where(low_rows, left, pltpu.roll(right, 4, 0))
            second = jnp.where(low_rows, pltpu.roll(left, 4, 0), right)
            tile = jnp.concatenate([first, second], 0).astype(jnp.bfloat16)
            for day_side in range(2):
                start = (day_side * half + slow * (FAST // 2) + 2 * pair) * 8
                sent[start : start + 16, :] = tile


def sum_kernel(received, out):
    rows = received.shape[0] // NSRC
    for source in range(NSRC):
        sums = [None] * 8
        for place in range(rows // 16):
            term = received[source * rows + place * 16 : source * rows + (place + 1) * 16, :].astype(jnp.float32)
            sums[place % 8] = term if place < 8 else sums[place % 8] + term
        while len(sums) > 1:
            sums = [first + second for first, second in zip(sums[::2], sums[1::2])]
        total = sums[0][:8] + sums[0][8:]
        for row in range(8):
            upper, slow, part = row // 4, row // 2 % 2, row % 2
            out[slow, source, part, upper * LANES : (upper + 1) * LANES] = total[row]


def in_hbm(array):
    return pltpu.with_memory_space_constraint(array, pltpu.HBM)


def shards(spectra, sources, offsets):
    windows = spectra.shape[0]
    width = spectra.shape[2]
    peers = lax.axis_size("days") * lax.axis_size("chan")
    all_windows = windows * lax.axis_size("days")
    channels = width * lax.axis_size("chan")
    scale = all_windows**1.5 / math.sqrt(channels) / all_windows**3
    scale /= math.sqrt(LAGS)
    forward = forward_table(scale)
    vmem = pl.BlockSpec(memory_space=pltpu.VMEM)
    far = pl.BlockSpec(memory_space=pltpu.HBM)
    block = windows * 2 * BINS // LANES

    other = lax.ppermute(spectra, "days", [(0, 1), (1, 0)])
    inverse = jnp.asarray(inverse_table())
    forward = jnp.asarray(forward)
    candidates, steep, rotor, own, inverse, forward = pl.pallas_call(
        front_kernel,
        out_shape=(
            jax.ShapeDtypeStruct((peers * block, LANES), jnp.bfloat16),
            jax.ShapeDtypeStruct((GROUPS // 2, 2 * LANES, 2 * LANES), jnp.bfloat16),
            jax.ShapeDtypeStruct((2, BINS, LANES), jnp.float32),
            jax.ShapeDtypeStruct(spectra.shape, jnp.bfloat16),
            jax.ShapeDtypeStruct(inverse.shape, jnp.bfloat16),
            jax.ShapeDtypeStruct(forward.shape, jnp.bfloat16),
        ),
        in_specs=[far] * 5,
        out_specs=(vmem,) * 6,
        scratch_shapes=[
            pltpu.VMEM((1, NSRC), jnp.int32),
            pltpu.VMEM((1, width), jnp.int32),
            pltpu.SemaphoreType.DMA((5,)),
        ],
        name="front",
        compiler_params=pltpu.CompilerParams(vmem_limit_bytes=8 << 20),
    )(
        in_hbm(sources.reshape(1, NSRC)),
        in_hbm(offsets.reshape(1, width)),
        in_hbm(spectra),
        in_hbm(inverse),
        in_hbm(forward),
    )
    received = lax.all_to_all(candidates.reshape(peers, block, LANES), BOTH, 0, 0, tiled=True)
    received = received.reshape(peers * block, LANES)
    terms = pl.pallas_call(
        functools.partial(main_kernel, scale),
        out_shape=jax.ShapeDtypeStruct((peers * 8, LANES), jnp.bfloat16),
        in_specs=[vmem] * 7,
        out_specs=vmem,
        scratch_shapes=[
            pltpu.VMEM((all_windows, LAGS, 2 * LANES), jnp.float32),
            pltpu.VMEM((LAGS, 2 * LANES), jnp.bfloat16),
            pltpu.VMEM((GROUPS, 2 * FAST * GROUP, LANES), jnp.float32),
        ],
        name="stack_and_slant",
        compiler_params=pltpu.CompilerParams(vmem_limit_bytes=24 << 20),
    )(received, own, other, steep, rotor, inverse, forward)
    partial = lax.all_to_all(terms.reshape(peers, 8, LANES), BOTH, 0, 0, tiled=True)
    return pl.pallas_call(
        sum_kernel,
        out_shape=jax.ShapeDtypeStruct((NSLOW // lax.axis_size("chan"), NSRC, 2, BINS), jnp.float32),
        in_specs=[vmem],
        out_specs=vmem,
        name="sum",
        compiler_params=pltpu.CompilerParams(vmem_limit_bytes=8 << 20),
    )(partial.reshape(peers * 8, LANES))


def solution(mesh):
    placed = (P("days", None, "chan"), P(), P("chan"))
    return jax.shard_map(
        shards, mesh=mesh, in_specs=placed, out_specs=P("chan", None, None, None), check_vma=False
    )
```
